32 devices in a mesh: band: 4 (over z), tile: 8 (over y, x, core).
Axes of the slice: x: 2, y: 2, z: 4, core: 2. Of those that a mesh axis runs over, the one named last changes fastest.
Arguments:
- pixel_map: bfloat16 [4, 384, 4, 128], P('band', 'tile'), may hold values from -6 to 6
- interp_bands: bfloat16 [2, 2, 128, 128], replicated, may hold values from -0.375 to 0.375
- conv1_weight: bfloat16 [16, 4, 3, 3], replicated, may hold values from -1 to 1
- conv1_bias: float32 [16], replicated, may hold values from -3 to 3
- conv2_weight: bfloat16 [16, 16, 3, 3], replicated, may hold values from -0.5 to 0.5
- send_rows: int32 [4, 8, 8, 32], P('band', 'tile'), may hold values from 0 to 47
- patch_slots: int32 [4, 8, 129], P('band', 'tile'), may hold values from 0 to 255
- patch_rows: int32 [4, 8], P('band', 'tile'), may hold values from 64 to 128, as said below
- cotangent: bfloat16 [4, 8, 16, 128, 128], P('band', 'tile'), may hold values from -18 to 18
Outputs:
- grad_map: float32 [4, 384, 4, 128], P('band', 'tile')
- grad_conv1: float32 [16, 4, 3, 3], replicated
- grad_bias: float32 [16], replicated
- grad_conv2: float32 [16, 16, 3, 3], replicated
The draws below stay inside these ranges and needn't reach their ends.
Inputs may be any that keep to these rules, and one draw needn't show every extreme that they name: `patch_rows`: every draw has a patch with all 128 rows valid.
All inputs are finite; a program needn't handle non-finite values.
Results may differ from the reference program's by a relative error of at most 0.0044.
Values may be sent and summed in bfloat16 or wider, within the bound.
No kernel may reach another device: no remote copies, remote signals or barrier semaphores. Data moves between devices by JAX's collectives and lax.ppermute only.
A program may use at most 128 MiB of HBM per device.

```python
import jax
import jax.numpy as jnp
from jax import lax

FREQ = 4
C1 = 16
C2 = 16
S = 128
NBLK = 48
P_DEV = 1
RECV = 256
NSRC = 129
CAP = 32
BLOCKS_BAND = 384
PATCH_BAND = 8
N_BAND = 4
N_TILE = 8


def draw_patch_rows(key, part):
    values = jax.random.randint(key, (N_BAND, PATCH_BAND), S // 2, S + 1, dtype=jnp.int32)
    return values.at[0, 0].set(S)


def draw_cotangent(key, part):
    key_noise = jax.random.fold_in(key, 0)
    key_scale = jax.random.fold_in(key, 2)
    normal_part = jax.random.normal(key_noise, (N_BAND, PATCH_BAND, C2, S, S), jnp.float32)
    position = jnp.arange(N_BAND * PATCH_BAND, dtype=jnp.float32).reshape(N_BAND, PATCH_BAND) / max(N_BAND * PATCH_BAND - 1, 1)
    jitter = jax.random.uniform(key_scale, (N_BAND, PATCH_BAND), jnp.float32, 0.7, 1.4)
    factor = jnp.exp(position * 1.0986123) * jitter
    values = jnp.clip(normal_part * factor[:, :, None, None, None], -18.0, 18.0)
    return values.astype(jnp.bfloat16)


def touch_ends(values, stream_key, low, top_value):
    longest = values.shape.index(max(values.shape))
    spots = []
    for shift in (0, 1):
        where = [jax.random.randint(jax.random.fold_in(stream_key, axis), (), 0, length) for axis, length in enumerate(values.shape)]
        where[longest] = (where[longest] + shift) % values.shape[longest]
        spots.append(tuple(where))
    return values.at[spots[0]].set(low).at[spots[1]].set(top_value)


def block_levels(stream_key, extent, pieces, low, top_value):
    loudness = 1.0
    for dim, blocks in pieces:
        heights = jax.random.uniform(jax.random.fold_in(jax.random.fold_in(stream_key, 6), dim), (blocks,), jnp.float32, low / len(pieces), top_value / len(pieces))
        loudness = loudness * jnp.repeat(jnp.exp(heights), extent[dim] // blocks).reshape((-1,) + (1,) * (len(extent) - 1 - dim))
    return loudness


def gaussian(own_key, shape, scale, limit, pieces=(), held_as=jnp.bfloat16):
    entries = scale * jax.random.normal(own_key, shape, jnp.float32)
    if pieces:
        entries = entries * block_levels(own_key, shape, pieces, -0.22, 0.18)
    return jnp.clip(entries, -limit, limit).astype(held_as)


def setup_inputs(seed: int = 0) -> dict:
    arg_keys = jax.random.split(jax.random.key(seed), 10)
    pixel_map = gaussian(arg_keys[0], (N_BAND, BLOCKS_BAND, FREQ, S), 1.0, 6.0, ((0, 4), (1, 8)))
    interp_bands = gaussian(arg_keys[1], (2, 2, S, S), (2 * S) ** -0.5, 0.375)
    conv1_weight = gaussian(arg_keys[2], (C1, FREQ, 3, 3), (9 * FREQ) ** -0.5, 1.0)
    conv1_bias = gaussian(arg_keys[3], (C1,), 0.5, 3.0, (), jnp.float32)
    conv2_weight = gaussian(arg_keys[4], (C2, C1, 3, 3), (9 * C1) ** -0.5, 0.5)
    send_rows = touch_ends(jax.random.randint(arg_keys[5], (N_BAND, N_TILE, N_TILE, CAP), 0, NBLK), jax.random.fold_in(arg_keys[5], 1), 0, NBLK - 1).astype(jnp.int32)
    patch_slots = touch_ends(jax.random.randint(arg_keys[6], (N_BAND, PATCH_BAND, NSRC), 0, RECV), jax.random.fold_in(arg_keys[6], 1), 0, RECV - 1).astype(jnp.int32)
    patch_rows = draw_patch_rows(jax.random.fold_in(arg_keys[9], 71), 0)
    cotangent = draw_cotangent(jax.random.fold_in(arg_keys[9], 71), 0)
    return dict(pixel_map=pixel_map, interp_bands=interp_bands, conv1_weight=conv1_weight, conv1_bias=conv1_bias, conv2_weight=conv2_weight, send_rows=send_rows, patch_slots=patch_slots, patch_rows=patch_rows, cotangent=cotangent)


def conv_same(images, kernel):
    return lax.conv_general_dilated(images, kernel, (1, 1), ((1, 1), (1, 1)), dimension_numbers=('NCHW', 'OIHW', 'NCHW'), preferred_element_type=jnp.float32)

def kernel_grad(images, upstream):
    result = lax.conv_general_dilated(images, upstream, (1, 1), ((1, 1), (1, 1)), dimension_numbers=('CNHW', 'IOHW', 'NCHW'), preferred_element_type=jnp.float32)
    return jnp.transpose(result, (1, 0, 2, 3))

def flipped(weights):
    return jnp.flip(jnp.transpose(weights, (1, 0, 2, 3)), (2, 3))

def patch_grads(sources, matrices, row_valid, upstream, conv1_weight, conv1_bias, conv2_weight):
    patch_count, row_length = (sources.shape[0], sources.shape[3])
    paired = jnp.concatenate([sources[:, :-1], sources[:, 1:]], axis=3)
    stacked = matrices.reshape(2 * row_length, row_length)
    rows_out = jnp.dot(paired.reshape(-1, 2 * row_length), stacked, preferred_element_type=jnp.float32)
    rows_out = rows_out.reshape(patch_count, row_length, -1, row_length)
    rows_out = jnp.where(row_valid[:, :, None, None], rows_out, 0.0)
    patch_image = jnp.transpose(rows_out.astype(jnp.bfloat16), (0, 2, 1, 3))
    pre_act = conv_same(patch_image, conv1_weight) + conv1_bias[None, :, None, None]
    gating = jax.nn.sigmoid(pre_act)
    hidden = (pre_act * gating).astype(jnp.bfloat16)
    grad_w2 = kernel_grad(hidden, upstream)
    grad_hidden = conv_same(upstream, flipped(conv2_weight))
    grad_pre = (grad_hidden * gating * (1.0 + pre_act * (1.0 - gating))).astype(jnp.bfloat16)
    grad_w1 = kernel_grad(patch_image, grad_pre)
    grad_b1 = lax.optimization_barrier(jnp.sum(grad_pre, axis=(0, 2, 3), dtype=jnp.float32))
    grad_image = conv_same(grad_pre, flipped(conv1_weight))
    grad_rows = jnp.transpose(grad_image, (0, 2, 1, 3))
    grad_rows = jnp.where(row_valid[:, :, None, None], grad_rows, 0.0).astype(jnp.bfloat16)
    paired_grad = jnp.dot(grad_rows.reshape(-1, row_length), stacked.T, preferred_element_type=jnp.float32)
    paired_grad = paired_grad.reshape(patch_count, row_length, -1, 2 * row_length)
    lower = paired_grad[..., :row_length]
    higher = paired_grad[..., row_length:]
    zero_row = jnp.zeros_like(lower[:, :1])
    grad_src = jnp.concatenate([lower, zero_row], axis=1) + jnp.concatenate([zero_row, higher], axis=1)
    return (grad_src, grad_w1, grad_b1, grad_w2)

def take_rows(table, picks):
    return jnp.take(table, picks, axis=0)

def reference(pixel_map, interp_bands, conv1_weight, conv1_bias, conv2_weight, send_rows, patch_slots, patch_rows, cotangent):
    band_numbers = jnp.arange(N_BAND, dtype=jnp.int32)

    def band_terms(inputs):
        band_map, band_lists, band_slots, band_rows, band_cot, band_number = inputs
        offsets = NBLK * jnp.arange(N_TILE, dtype=jnp.int32)
        flat_ids = band_lists + offsets[:, None, None]
        flat_ids = jnp.transpose(flat_ids, (1, 0, 2)).reshape(N_TILE, RECV)
        slot_grid = band_slots.reshape(N_TILE, P_DEV, S + 1)
        block_ids = jax.vmap(take_rows)(flat_ids, slot_grid).reshape(-1)
        sources = jnp.take(band_map, block_ids, axis=0).reshape(PATCH_BAND, S + 1, FREQ, S)
        is_polar = jnp.logical_or(band_number < N_BAND // 4, band_number >= N_BAND - N_BAND // 4)
        matrices = jnp.where(is_polar, interp_bands[0], interp_bands[1])
        row_valid = jnp.arange(S)[None, :] < band_rows[:, None]
        grad_src, grad_w1, grad_b1, grad_w2 = patch_grads(sources, matrices, row_valid, band_cot, conv1_weight, conv1_bias, conv2_weight)
        band_grad = jax.ops.segment_sum(grad_src.reshape(-1, FREQ, S), block_ids, num_segments=BLOCKS_BAND)
        return (band_grad, grad_w1, grad_b1, grad_w2)
    band_grads, w1_terms, b1_terms, w2_terms = lax.map(band_terms, (pixel_map, send_rows, patch_slots, patch_rows, cotangent, band_numbers))
    norm_scale = float(N_BAND * PATCH_BAND * S * S) ** (-0.5)
    return (band_grads, lax.optimization_barrier(jnp.sum(w1_terms, axis=0)) * norm_scale, lax.optimization_barrier(jnp.sum(b1_terms, axis=0)) * norm_scale, lax.optimization_barrier(jnp.sum(w2_terms, axis=0)) * norm_scale)
```

```python
import functools

import jax
import jax.numpy as jnp
from jax import lax
from jax.experimental import pallas as pl
from jax.experimental.pallas import tpu as pltpu
from jax.sharding import PartitionSpec as P

BF = jnp.bfloat16
F32 = jnp.float32
I32 = jnp.int32
S = 128
FREQ = 4
CH = 16
R = 8
NB = S // R
WIN = (R + 2) * CH
XW = 48
LANES = NB * S
SRC = 144
VMEM_LIMIT = 48 * 1024 * 1024


def iota(shape, axis):
    return lax.broadcasted_iota(I32, shape, axis)


def dot(a, b):
    return lax.dot_general(a, b, (((1,), (0,)), ((), ())), preferred_element_type=F32)


def dot_t(a, b):
    return lax.dot_general(a, b, (((1,), (1,)), ((), ())), preferred_element_type=F32)


def third(k):
    return (k * 171) >> 9


def shifted(rows, step):
    lane = iota(rows.shape, 1)
    if step == 1:
        return jnp.where(lane == S - 1, 0.0, pltpu.roll(rows, S - 1, 1))
    return jnp.where(lane == 0, 0.0, pltpu.roll(rows, 1, 1))


def store_window(ref, base, y, tile):
    block, r = divmod(y, R)
    ref[base + (r + 1) * CH : base + (r + 2) * CH, block * S : (block + 1) * S] = tile
    if r == 0 and block > 0:
        ref[base + (R + 1) * CH : base + WIN, (block - 1) * S : block * S] = tile
    if r == R - 1 and block < NB - 1:
        ref[base : base + CH, (block + 1) * S : (block + 2) * S] = tile


def zero_edges(ref, base):
    zero = jnp.zeros((CH, S), BF)
    ref[base : base + CH, 0:S] = zero
    ref[base + (R + 1) * CH : base + WIN, LANES - S : LANES] = zero


def outgoing_kernel(rows_ref, map_ref, out_ref):
    owners, capacity = rows_ref.shape
    for t in range(owners):
        for c in range(capacity):
            out_ref[t * capacity + c] = map_ref[rows_ref[t, c]]


def prepare_kernel(
    polar_ref,
    cot_ref,
    w1_ref,
    w1t_ref,
    w2t_ref,
    bias_ref,
    interp_ref,
    slots_ref,
    send_ref,
    cb_ref,
    gh_ref,
    t1_ref,
    bcol_ref,
    t3_ref,
    ms_ref,
    mt_ref,
    oh_ref,
    sel_ref,
    plane,
    lists,
    t2_ref,
):
    owners, capacity = send_ref.shape
    chunk = capacity + CH
    nsrc = slots_ref.shape[1]
    for o in range(CH):
        plane[o * S : (o + 1) * S, :] = cot_ref[o * S : (o + 1) * S, :].astype(F32)
    for dx in range(3):
        zero_edges(cb_ref, dx * WIN)
    for y in range(S):
        rows = plane[pl.ds(y, CH, stride=S), :]
        store_window(cb_ref, 0, y, shifted(rows, 1).astype(BF))
        store_window(cb_ref, WIN, y, rows.astype(BF))
        store_window(cb_ref, 2 * WIN, y, shifted(rows, -1).astype(BF))

    pick = ((iota((R * CH, CH), 0) & 15) == iota((R * CH, CH), 1)).astype(BF)
    spread = dot(pick, w2t_ref[...]).astype(BF)
    row, col = iota((R * CH, 3 * WIN), 0), iota((R * CH, 3 * WIN), 1)
    gap = ((col - jnp.where(col >= 2 * WIN, 2 * WIN, jnp.where(col >= WIN, WIN, 0))) >> 4) - (row >> 4)
    k, kcol = iota((CH * 9, 3 * WIN), 0), iota((CH * 9, 3 * WIN), 1)
    kdx = jnp.where(kcol >= 2 * WIN, 2, jnp.where(kcol >= WIN, 1, 0))
    source = (kcol & 15) * 9 + kdx
    banded = jnp.zeros((R * CH, 3 * WIN), F32)
    for dy in range(3):
        term = dot(spread, (k == source + dy * 3).astype(BF))
        banded = jnp.where(gap == 2 - dy, term, banded)
    t2_ref[...] = banded.astype(BF)
    for n in range(0, LANES, 512):
        gh_ref[:, n : n + 512] = dot(t2_ref[...], cb_ref[:, n : n + 512])

    spread = dot(pick, w1_ref[...]).astype(BF)
    width = 3 * XW + CH
    row, col = iota((R * CH, width), 0), iota((R * CH, width), 1)
    cdx = jnp.where(col >= 3 * XW, 3, jnp.where(col >= 2 * XW, 2, jnp.where(col >= XW, 1, 0)))
    gap = ((col - cdx * XW) >> 2) - (row >> 4)
    gap = jnp.where(cdx == 3, -1, gap)
    k, kcol = iota((FREQ * 9, width), 0), iota((FREQ * 9, width), 1)
    kdx = jnp.where(kcol >= 3 * XW, 3, jnp.where(kcol >= 2 * XW, 2, jnp.where(kcol >= XW, 1, 0)))
    source = (kcol & 3) * 9 + kdx
    banded = jnp.zeros((R * CH, width), F32)
    for dy in range(3):
        term = dot(spread, (k == source + dy * 3).astype(BF))
        banded = jnp.where(gap == dy, term, banded)
    t1_ref[...] = banded.astype(BF)
    where_bias = (iota((R * CH, CH), 0) & 15) == iota((R * CH, CH), 1)
    column = jnp.sum(jnp.where(where_bias, bias_ref[...], 0.0), axis=1, keepdims=True)
    bcol_ref[...] = jnp.broadcast_to(column, (R * CH, S))

    part = R * FREQ
    tall = 3 * part
    pick = ((iota((tall, FREQ), 0) & 3) == iota((tall, FREQ), 1)).astype(BF)
    spread = dot(pick, w1t_ref[...])
    row, k = iota((tall, CH * 9), 0), iota((tall, CH * 9), 1)
    rdx = jnp.where(row >= 2 * part, 2, jnp.where(row >= part, 1, 0))
    spread = jnp.where(k - 3 * third(k) == rdx, spread, 0.0).astype(BF)
    row, col = iota((tall, WIN), 0), iota((tall, WIN), 1)
    gap = (col >> 4) - ((row & (part - 1)) >> 2)
    k, kcol = third(iota((CH * 9, WIN), 0)), iota((CH * 9, WIN), 1)
    banded = jnp.zeros((tall, WIN), F32)
    for dy in range(3):
        term = dot(spread, (k == (kcol & 15) * 3 + dy).astype(BF))
        banded = jnp.where(gap == 2 - dy, term, banded)
    t3_ref[...] = banded.astype(BF)

    for half in range(2):
        matrix = jnp.where(
            polar_ref[0] == 1, interp_ref[0, half].astype(F32), interp_ref[1, half].astype(F32)
        )
        at = slice(half * S, (half + 1) * S)
        ms_ref[at, 0:S] = shifted(matrix, -1).astype(BF)
        ms_ref[at, S : 2 * S] = matrix.astype(BF)
        ms_ref[at, 2 * S : 3 * S] = shifted(matrix, 1).astype(BF)
        mt_ref[at, :] = matrix.T.astype(BF)

    slots = jnp.concatenate([slots_ref[...], jnp.full((1, SRC - nsrc), -1, I32)], axis=1)
    for t in range(owners):
        c = iota((chunk, SRC), 0)
        hit = (c + t * capacity == slots) & (c < capacity)
        oh_ref[t * chunk : (t + 1) * chunk, :] = jnp.where(hit, 1.0, 0.0).astype(BF)
        lists[0:1, t * chunk : t * chunk + capacity] = send_ref[t : t + 1, :]
        lists[0:1, t * chunk + capacity : (t + 1) * chunk] = (
            iota((1, CH), 1) + sel_ref.shape[0] - CH
        )
    hit = lists[...] == iota(sel_ref.shape, 0)
    sel_ref[...] = jnp.where(hit, 1.0, 0.0).astype(BF)


def patch_kernel(
    slots_ref,
    rows_ref,
    recv_ref,
    ms_ref,
    t1_ref,
    bcol_ref,
    gh_ref,
    cb_ref,
    w_ref,
    gp_ref,
    src,
    img,
    xb,
    hb,
):
    nsrc = slots_ref.shape[1]
    total = src.shape[0]
    src[0:FREQ, :] = jnp.zeros((FREQ, S), F32)
    first = FREQ * (nsrc + 1)
    src[first:total, :] = jnp.zeros((total - first, S), F32)
    for k in range(nsrc):
        src[FREQ * (k + 1) : FREQ * (k + 2), :] = recv_ref[slots_ref[0, k]].astype(F32)
    limit = FREQ * (rows_ref[0, 0] + 1)
    step = img.shape[1] // 3
    for a in range(0, img.shape[1], step):
        pair = jnp.concatenate([src[a : a + step, :], src[a + FREQ : a + FREQ + step, :]], axis=1)
        out = dot(pair.astype(BF), ms_ref[...])
        at = iota(out.shape, 0) + a
        out = jnp.where((at >= FREQ) & (at < limit), out, 0.0).astype(BF)
        for dx in range(3):
            img[dx, a : a + step, :] = out[:, dx * S : (dx + 1) * S]
    for m in range(NB):
        for dx in range(3):
            xb[dx * XW : (dx + 1) * XW, m * S : (m + 1) * S] = img[
                dx, m * R * FREQ : m * R * FREQ + XW, :
            ]
    xb[3 * XW :, :] = jnp.ones((CH, LANES), BF)
    zero_edges(hb, 0)
    zero_edges(gp_ref, 0)
    bias = jnp.concatenate([bcol_ref[...], bcol_ref[...]], axis=1)
    for n in range(0, LANES, 2 * S):
        pre = dot(t1_ref[...], xb[:, n : n + 2 * S]) + bias
        gate = jax.nn.sigmoid(pre)
        hidden = (pre * gate).astype(BF)
        grad = (gh_ref[:, n : n + 2 * S] * (gate * (1.0 + pre * (1.0 - gate)))).astype(BF)
        for b in range(2):
            m = n // S + b
            lanes = slice(b * S, (b + 1) * S)
            for ref, value in ((hb, hidden), (gp_ref, grad)):
                ref[CH : CH + R * CH, m * S : (m + 1) * S] = value[:, lanes]
                if m > 0:
                    ref[(R + 1) * CH : WIN, (m - 1) * S : m * S] = value[0:CH, lanes]
                if m < NB - 1:
                    ref[0:CH, (m + 1) * S : (m + 2) * S] = value[(R - 1) * CH :, lanes]
    lane = iota((CH, 2 * S), 1)
    result = jnp.zeros((CH, 2 * S), F32)
    for dx in range(3):
        g = dot_t(cb_ref[dx * WIN + CH : dx * WIN + CH + R * CH, :], hb[...])
        g = jnp.concatenate([g, jnp.zeros((R * CH, 2 * S - WIN), F32)], axis=1)
        acc = g[0:CH, :]
        for r in range(1, R):
            acc = acc + pltpu.roll(g[r * CH : (r + 1) * CH, :], 2 * S - r * CH, 1)
        if dx:
            acc = pltpu.roll(acc, dx * 3 * CH, 1)
        result = jnp.where((lane >= dx * 3 * CH) & (lane < (dx + 1) * 3 * CH), acc, result)
    g = dot_t(gp_ref[CH : CH + R * CH, :], xb[...])
    g = jnp.concatenate([g, jnp.zeros((R * CH, 2 * S - g.shape[1]), F32)], axis=1)
    acc = g[0:CH, :]
    ones = g[0:CH, :]
    for r in range(1, R):
        part = g[r * CH : (r + 1) * CH, :]
        ones = ones + part
        acc = acc + pltpu.roll(part, 2 * S - r * FREQ, 1)
    acc = pltpu.roll(acc, 9 * CH, 1)
    ones = pltpu.roll(ones, 2 * S - 1 - 3 * XW, 1)
    result = jnp.where(lane >= 9 * CH, acc, result)
    w_ref[...] = jnp.where(lane == 2 * S - 1, ones, result)


def slots_kernel(rows_ref, gp_ref, t3_ref, mt_ref, oh_ref, out_ref, grad, gsrc):
    part = R * FREQ
    limit = rows_ref[0, 0]
    pad = 2 * FREQ
    grad[0:pad, :] = jnp.zeros((pad, S), F32)
    end = pad + S * FREQ
    grad[end:, :] = jnp.zeros((grad.shape[0] - end, S), F32)
    for n in range(0, LANES, 4 * S):
        u = dot(t3_ref[...], gp_ref[:, n : n + 4 * S])
        for b in range(4):
            m = n // S + b
            lanes = slice(b * S, (b + 1) * S)
            rows = shifted(u[0:part, lanes], 1) + u[part : 2 * part, lanes]
            rows = rows + shifted(u[2 * part : 3 * part, lanes], -1)
            y = (iota(rows.shape, 0) >> 2) + m * R
            grad[pad + m * part : pad + (m + 1) * part, :] = jnp.where(y < limit, rows, 0.0)
    step = 176
    for a in range(0, 3 * step, step):
        pair = jnp.concatenate(
            [grad[pad + a : pad + a + step, :], grad[FREQ + a : FREQ + a + step, :]], axis=1
        )
        gsrc[a : a + step, :] = dot(pair.astype(BF), mt_ref[...])
    gsrc[3 * step :, :] = jnp.zeros((gsrc.shape[0] - 3 * step, S), F32)
    for f in range(FREQ):
        rows = gsrc[pl.ds(f, SRC, stride=FREQ), :]
        high = rows.astype(BF)
        low = (rows - high.astype(F32)).astype(BF)
        out = dot(oh_ref[...], high) + dot(oh_ref[...], low)
        out_ref[:, f * S : (f + 1) * S] = out.astype(BF)


def pack_kernel(w_ref, buffer_ref, out_ref, packed, sems):
    del buffer_ref
    owners, chunk, _ = out_ref.shape
    total = w_ref[...]
    high = total.astype(BF)
    packed[:, 0 : 2 * S] = high
    packed[:, 2 * S : 4 * S] = (total - high.astype(F32)).astype(BF)
    copies = [
        pltpu.make_async_copy(packed, out_ref.at[t, pl.ds(chunk - CH, CH), :], sems.at[t])
        for t in range(owners)
    ]
    for copy in copies:
        copy.start()
    for copy in copies:
        copy.wait()


def final_kernel(scale, sel_ref, back_ref, map_ref, w_ref):
    blocks = map_ref.shape[0]
    total = dot(sel_ref[...], back_ref[...])
    for f in range(FREQ):
        map_ref[:, f, :] = total[0:blocks, f * S : (f + 1) * S]
    w_ref[...] = (total[blocks:, 0 : 2 * S] + total[blocks:, 2 * S : 4 * S]) * scale


def vmem(n):
    return [pl.BlockSpec(memory_space=pltpu.VMEM)] * n


def smem(n):
    return [pl.BlockSpec(memory_space=pltpu.SMEM)] * n


def call(kernel, out_shape, in_specs, out_specs, scratch=(), **extra):
    return pl.pallas_call(
        kernel,
        out_shape=out_shape,
        in_specs=in_specs,
        out_specs=out_specs,
        scratch_shapes=list(scratch),
        compiler_params=pltpu.CompilerParams(vmem_limit_bytes=VMEM_LIMIT),
        **extra,
    )


def arr(shape, dtype):
    return jax.ShapeDtypeStruct(shape, dtype)


def band_sum(value, count):
    if count & (count - 1):
        return lax.psum(value, "band")
    step = 1
    while step < count:
        pairs = [(i, i ^ step) for i in range(count)]
        value = value + lax.ppermute(value, "band", pairs)
        step *= 2
    return value


def shards(
    pixel_map,
    interp_bands,
    conv1_weight,
    conv1_bias,
    conv2_weight,
    send_rows,
    patch_slots,
    patch_rows,
    cotangent,
):
    tile_count = lax.axis_size("tile")
    band_count = lax.axis_size("band")
    band_index = lax.axis_index("band")
    owned = pixel_map[0]
    blocks = owned.shape[0]
    send = send_rows[0, 0]
    capacity = send.shape[1]
    chunk = capacity + CH
    slots = patch_slots[0]
    cot = cotangent.reshape(CH * S, S)

    outgoing = call(
        outgoing_kernel,
        arr((tile_count * capacity, FREQ, S), BF),
        smem(1) + vmem(1),
        vmem(1)[0],
    )(send, owned)
    received = lax.all_to_all(outgoing, "tile", split_axis=0, concat_axis=0, tiled=True)

    is_polar = jnp.logical_or(
        band_index < band_count // 4, band_index >= band_count - band_count // 4
    )
    polar = is_polar.astype(I32).reshape(1)
    w1 = conv1_weight.reshape(CH, FREQ * 9)
    w1t = jnp.transpose(conv1_weight, (1, 0, 2, 3)).reshape(FREQ, CH * 9)
    w2t = jnp.transpose(conv2_weight, (1, 0, 2, 3)).reshape(CH, CH * 9)
    cb, gh, t1, bcol, t3, ms, mt, oh, sel = call(
        prepare_kernel,
        (
            arr((3 * WIN, LANES), BF),
            arr((R * CH, LANES), F32),
            arr((R * CH, 3 * XW + CH), BF),
            arr((R * CH, S), F32),
            arr((3 * R * FREQ, WIN), BF),
            arr((2 * S, 3 * S), BF),
            arr((2 * S, S), BF),
            arr((tile_count * chunk, SRC), BF),
            arr((blocks + CH, tile_count * chunk), BF),
        ),
        smem(1) + vmem(8),
        vmem(9),
        (
            pltpu.VMEM((CH * S, S), F32),
            pltpu.VMEM((1, tile_count * chunk), I32),
            pltpu.VMEM((R * CH, 3 * WIN), BF),
        ),
        cost_estimate=pl.CostEstimate(flops=4 * 10**9, bytes_accessed=4 * 10**6, transcendentals=0),
    )(polar, cot, w1, w1t, w2t, conv1_bias.reshape(1, CH), interp_bands, slots, send)

    padded = (S + 4) * FREQ
    weights, gp = call(
        patch_kernel,
        (arr((CH, 2 * S), F32), arr((WIN, LANES), BF)),
        smem(2) + vmem(6),
        vmem(2),
        (
            pltpu.VMEM((padded + 8, S), F32),
            pltpu.VMEM((3, padded, S), BF),
            pltpu.VMEM((3 * XW + CH, LANES), BF),
            pltpu.VMEM((WIN, LANES), BF),
        ),
    )(slots, patch_rows, received, ms, t1, bcol, gh, cb)

    returning = call(
        slots_kernel,
        arr((tile_count * chunk, 4 * S), BF),
        smem(1) + vmem(4),
        vmem(1)[0],
        (pltpu.VMEM((padded + 16, S), F32), pltpu.VMEM((SRC * FREQ, S), F32)),
    )(patch_rows, gp, t3, mt, oh)
    weights = band_sum(weights, band_count)
    returning = call(
        pack_kernel,
        arr((tile_count, chunk, 4 * S), BF),
        vmem(1) + [pl.BlockSpec(memory_space=pl.ANY)],
        pl.BlockSpec(memory_space=pl.ANY),
        (pltpu.VMEM((CH, 4 * S), BF), pltpu.SemaphoreType.DMA((tile_count,))),
        input_output_aliases={1: 0},
    )(weights, returning.reshape(tile_count, chunk, 4 * S))
    returned = lax.all_to_all(returning, "tile", split_axis=0, concat_axis=0, tiled=True)
    norm_scale = float(band_count * tile_count * S * S) ** (-0.5)
    grad_map, total = call(
        functools.partial(final_kernel, norm_scale),
        (arr((blocks, FREQ, S), F32), arr((CH, 2 * S), F32)),
        vmem(2),
        vmem(2),
    )(sel, returned.reshape(tile_count * chunk, 4 * S))

    grad2 = total[:, 0 : 9 * CH].reshape(CH, 3, 3, CH)
    grad1 = jnp.stack([total[:, 9 * CH + dx * XW :][:, 0 : 3 * FREQ] for dx in range(3)], axis=1)
    grad1 = grad1.reshape(CH, 3, 3, FREQ)
    return (
        grad_map[None],
        jnp.transpose(grad1, (0, 3, 2, 1)),
        total[:, 2 * S - 1],
        jnp.transpose(grad2, (0, 3, 2, 1)),
    )


def solution(mesh):
    in_specs = (
        P("band", "tile", None, None),
        P(),
        P(),
        P(),
        P(),
        P("band", "tile", None, None),
        P("band", "tile", None),
        P("band", "tile"),
        P("band", "tile", None, None, None),
    )
    out_specs = (P("band", "tile", None, None), P(), P(), P())
    return jax.shard_map(shards, mesh=mesh, in_specs=in_specs, out_specs=out_specs, check_vma=False)
```

```python
import functools

import jax
import jax.numpy as jnp
from jax import lax
from jax.experimental import pallas as pl
from jax.experimental.pallas import tpu as pltpu
from jax.sharding import PartitionSpec as P

BF = jnp.bfloat16
F32 = jnp.float32
I32 = jnp.int32
S = 128
FREQ = 4
CH = 16
R = 8
NB = S // R
WIN = (R + 2) * CH
XW = 48
LANES = NB * S
SRC = 144
VMEM_LIMIT = 16 * 1024 * 1024


def iota(shape, axis):
    return lax.broadcasted_iota(I32, shape, axis)


def dot(a, b):
    return lax.dot_general(a, b, (((1,), (0,)), ((), ())), preferred_element_type=F32)


def dot_t(a, b):
    return lax.dot_general(a, b, (((1,), (1,)), ((), ())), preferred_element_type=F32)


def shifted(rows, step):
    lane = iota(rows.shape, 1)
    if step == 1:
        return jnp.where(lane == S - 1, 0.0, pltpu.roll(rows, S - 1, 1))
    return jnp.where(lane == 0, 0.0, pltpu.roll(rows, 1, 1))


def store_window(ref, base, y, tile):
    block, r = divmod(y, R)
    ref[base + (r + 1) * CH : base + (r + 2) * CH, block * S : (block + 1) * S] = tile
    if r == 0 and block > 0:
        ref[base + (R + 1) * CH : base + WIN, (block - 1) * S : block * S] = tile
    if r == R - 1 and block < NB - 1:
        ref[base : base + CH, (block + 1) * S : (block + 2) * S] = tile


def zero_edges(ref, base):
    zero = jnp.zeros((CH, S), BF)
    ref[base : base + CH, 0:S] = zero
    ref[base + (R + 1) * CH : base + WIN, LANES - S : LANES] = zero


class View:
    def __init__(self, ref, row, rows, lane, lanes):
        self.ref, self.origin, self.shape = ref, (row, lane), (rows, lanes)

    def place(self, key):
        key = (slice(None), slice(None)) if key is Ellipsis else key
        spans = [k.indices(n) for k, n in zip(key, self.shape)]
        return tuple(slice(o + a, o + b) for o, (a, b, _) in zip(self.origin, spans))

    def __getitem__(self, key):
        return self.ref[self.place(key)]

    def __setitem__(self, key, value):
        self.ref[self.place(key)] = value


def early(ref):
    return View(ref, 2 * S, R * CH, LANES, 3 * XW + CH), View(ref, 0, 2 * S, LANES, 3 * S)


def late(ref, chunks, blocks):
    return (
        View(ref, 0, chunks, 0, SRC),
        View(ref, 0, 2 * S, 2 * S, S),
        View(ref, 2 * S, 3 * R * FREQ, 2 * S, WIN),
        View(ref, 0, blocks + CH, 4 * S, chunks),
    )


def fetch(pairs, sems):
    copies = [pltpu.make_async_copy(a, b, sems.at[i]) for i, (a, b) in enumerate(pairs)]
    for copy in copies:
        copy.start()
    return copies


def outgoing_kernel(send_hbm, map_hbm, out_ref, rows_ref, map_ref, sems):
    owners, capacity = rows_ref.shape
    for copy in fetch(((send_hbm, rows_ref), (map_hbm, map_ref)), sems):
        copy.wait()
    for t in range(owners):
        for c in range(capacity):
            out_ref[t * capacity + c] = map_ref[rows_ref[t, c]]


def prepare_kernel(
    polar_ref,
    cot_hbm,
    w1_hbm,
    w2_hbm,
    interp_hbm,
    big_ref,
    gh_ref,
    cb_ref,
    plane,
    t2_ref,
    cot_ref,
    w1_ref,
    w2_ref,
    interp_ref,
    stack1,
    stack2,
    sems,
):
    copies = fetch(
        ((w1_hbm, w1_ref), (w2_hbm, w2_ref), (interp_hbm, interp_ref), (cot_hbm, cot_ref)), sems
    )
    t1_ref, ms_ref = early(big_ref)
    for copy in copies[:-1]:
        copy.wait()
    for i in range(9):
        stack1[i * FREQ : (i + 1) * FREQ, :] = w1_ref[i].astype(F32)
        stack2[i * CH : (i + 1) * CH, :] = w2_ref[i].astype(F32)
    pick = ((iota((R * CH, CH), 0) & 15) == iota((R * CH, CH), 1)).astype(BF)
    spread = dot_t(pick, stack2[...].astype(BF)).astype(BF)
    row, col = iota((R * CH, 3 * WIN), 0), iota((R * CH, 3 * WIN), 1)
    gap = ((col - jnp.where(col >= 2 * WIN, 2 * WIN, jnp.where(col >= WIN, WIN, 0))) >> 4) - (row >> 4)
    k, kcol = iota((CH * 9, 3 * WIN), 0), iota((CH * 9, 3 * WIN), 1)
    kdx = jnp.where(kcol >= 2 * WIN, 2, jnp.where(kcol >= WIN, 1, 0))
    source = kdx * CH + (kcol & 15)
    banded = jnp.zeros((R * CH, 3 * WIN), F32)
    for dy in range(3):
        term = dot(spread, (k == source + dy * 3 * CH).astype(BF))
        banded = jnp.where(gap == 2 - dy, term, banded)
    t2_ref[...] = banded.astype(BF)
    weights1 = stack1[...].astype(BF)
    spread = dot_t(pick, weights1).astype(BF)
    width = 3 * XW + CH
    row, col = iota((R * CH, width), 0), iota((R * CH, width), 1)
    cdx = jnp.where(col >= 3 * XW, 3, jnp.where(col >= 2 * XW, 2, jnp.where(col >= XW, 1, 0)))
    gap = ((col - cdx * XW) >> 2) - (row >> 4)
    gap = jnp.where(cdx == 3, -1, gap)
    k, kcol = iota((FREQ * 9, width), 0), iota((FREQ * 9, width), 1)
    kdx = jnp.where(kcol >= 3 * XW, 3, jnp.where(kcol >= 2 * XW, 2, jnp.where(kcol >= XW, 1, 0)))
    source = kdx * FREQ + (kcol & 3)
    banded = jnp.zeros((R * CH, width), F32)
    for dy in range(3):
        term = dot(spread, (k == source + dy * 3 * FREQ).astype(BF))
        banded = jnp.where(gap == dy, term, banded)
    t1_ref[...] = banded.astype(BF)

    for half in range(2):
        matrix = jnp.where(
            polar_ref[0] == 1, interp_ref[0, half].astype(F32), interp_ref[1, half].astype(F32)
        )
        at = slice(half * S, (half + 1) * S)
        ms_ref[at, 0:S] = shifted(matrix, -1).astype(BF)
        ms_ref[at, S : 2 * S] = matrix.astype(BF)
        ms_ref[at, 2 * S : 3 * S] = shifted(matrix, 1).astype(BF)

    copies[-1].wait()
    for o in range(CH):
        plane[o * S : (o + 1) * S, :] = cot_ref[o * S : (o + 1) * S, :].astype(F32)
    for dx in range(3):
        zero_edges(cb_ref, dx * WIN)
    for y in range(S):
        rows = plane[pl.ds(y, CH, stride=S), :]
        block, r = divmod(y, R)
        for dx, tile in enumerate((shifted(rows, 1), rows, shifted(rows, -1))):
            tile = tile.astype(BF)
            store_window(cb_ref, dx * WIN, y, tile)
            at = dx * S + r * CH
            big_ref[at : at + CH, block * S : (block + 1) * S] = tile
    for n in range(0, LANES, 512):
        gh_ref[:, n : n + 512] = dot(t2_ref[...], cb_ref[:, n : n + 512])


def lists_kernel(
    blocks,
    polar_ref,
    w1_hbm,
    interp_hbm,
    slots_hbm,
    send_hbm,
    after_hbm,
    big_ref,
    lists,
    w1_ref,
    interp_ref,
    slots_ref,
    send_ref,
    stack1,
    sems,
):
    del after_hbm
    pairs = (
        (w1_hbm, w1_ref),
        (interp_hbm, interp_ref),
        (slots_hbm, slots_ref),
        (send_hbm, send_ref),
    )
    for copy in fetch(pairs, sems):
        copy.wait()
    owners, capacity = send_ref.shape
    chunk = capacity + CH
    nsrc = slots_ref.shape[1]
    oh_ref, mt_ref, t3_ref, sel_ref = late(big_ref, owners * chunk, blocks)
    for i in range(9):
        stack1[i * FREQ : (i + 1) * FREQ, :] = w1_ref[i].astype(F32)
    weights1 = stack1[...].astype(BF)
    part = R * FREQ
    tall = 3 * part
    row, k = iota((tall, FREQ * 9), 0), iota((tall, FREQ * 9), 1)
    rdx = jnp.where(row >= 2 * part, 2, jnp.where(row >= part, 1, 0))
    source = rdx * FREQ + (row & 3)
    column = ((iota((CH, WIN), 1) & 15) == iota((CH, WIN), 0)).astype(BF)
    row, col = iota((tall, WIN), 0), iota((tall, WIN), 1)
    gap = (col >> 4) - ((row & (part - 1)) >> 2)
    banded = jnp.zeros((tall, WIN), F32)
    for dy in range(3):
        spread = dot((k == source + dy * 3 * FREQ).astype(BF), weights1).astype(BF)
        banded = jnp.where(gap == 2 - dy, dot(spread, column), banded)
    t3_ref[...] = banded.astype(BF)

    for half in range(2):
        matrix = jnp.where(
            polar_ref[0] == 1, interp_ref[0, half].astype(F32), interp_ref[1, half].astype(F32)
        )
        mt_ref[half * S : (half + 1) * S, :] = matrix.T.astype(BF)

    slots = jnp.concatenate([slots_ref[...], jnp.full((1, SRC - nsrc), -1, I32)], axis=1)
    for t in range(owners):
        c = iota((chunk, SRC), 0)
        hit = (c + t * capacity == slots) & (c < capacity)
        oh_ref[t * chunk : (t + 1) * chunk, :] = jnp.where(hit, 1.0, 0.0).astype(BF)
        lists[0:1, t * chunk : t * chunk + capacity] = send_ref[t : t + 1, :]
        lists[0:1, t * chunk + capacity : (t + 1) * chunk] = (
            iota((1, CH), 1) + blocks
        )
    hit = lists[...] == iota(sel_ref.shape, 0)
    sel_ref[...] = jnp.where(hit, 1.0, 0.0).astype(BF)


def patch_kernel(
    slots_ref,
    rows_ref,
    bias_ref,
    recv_ref,
    big_ref,
    gh_ref,
    w_ref,
    gp_ref,
    src,
    img,
    xb,
    hb,
):
    nsrc = slots_ref.shape[1]
    total = src.shape[0]
    t1_ref, ms_ref = early(big_ref)
    src[0:FREQ, :] = jnp.zeros((FREQ, S), F32)
    first = FREQ * (nsrc + 1)
    src[first:total, :] = jnp.zeros((total - first, S), F32)
    for k in range(nsrc):
        src[FREQ * (k + 1) : FREQ * (k + 2), :] = recv_ref[slots_ref[0, k]].astype(F32)
    limit = FREQ * (rows_ref[0, 0] + 1)
    step = img.shape[1] // 3
    for a in range(0, img.shape[1], step):
        pair = jnp.concatenate([src[a : a + step, :], src[a + FREQ : a + FREQ + step, :]], axis=1)
        out = dot(pair.astype(BF), ms_ref[...])
        at = iota(out.shape, 0) + a
        out = jnp.where((at >= FREQ) & (at < limit), out, 0.0).astype(BF)
        for dx in range(3):
            img[dx, a : a + step, :] = out[:, dx * S : (dx + 1) * S]
    for m in range(NB):
        for dx in range(3):
            xb[dx * XW : (dx + 1) * XW, m * S : (m + 1) * S] = img[
                dx, m * R * FREQ : m * R * FREQ + XW, :
            ]
    xb[3 * XW :, :] = jnp.ones((CH, LANES), BF)
    zero_edges(hb, 0)
    zero_edges(gp_ref, 0)
    own = (iota((R * CH, CH), 0) & 15) == iota((R * CH, CH), 1)
    bias = jnp.sum(jnp.where(own, bias_ref[...], 0.0), axis=1, keepdims=True)
    for n in range(0, LANES, 2 * S):
        pre = dot(t1_ref[...], xb[:, n : n + 2 * S]) + bias
        gate = jax.nn.sigmoid(pre)
        hidden = (pre * gate).astype(BF)
        grad = (gh_ref[:, n : n + 2 * S] * (gate * (1.0 + pre * (1.0 - gate)))).astype(BF)
        for b in range(2):
            m = n // S + b
            lanes = slice(b * S, (b + 1) * S)
            for ref, value in ((hb, hidden), (gp_ref, grad)):
                ref[CH : CH + R * CH, m * S : (m + 1) * S] = value[:, lanes]
                if m > 0:
                    ref[(R + 1) * CH : WIN, (m - 1) * S : m * S] = value[0:CH, lanes]
                if m < NB - 1:
                    ref[0:CH, (m + 1) * S : (m + 2) * S] = value[(R - 1) * CH :, lanes]
    lane = iota((CH, 2 * S), 1)
    result = jnp.zeros((CH, 2 * S), F32)
    for dx in range(3):
        g = dot_t(big_ref[dx * S : (dx + 1) * S, 0:LANES], hb[...])
        g = jnp.concatenate([g, jnp.zeros((R * CH, 2 * S - WIN), F32)], axis=1)
        acc = g[0:CH, :]
        for r in range(1, R):
            acc = acc + pltpu.roll(g[r * CH : (r + 1) * CH, :], 2 * S - r * CH, 1)
        if dx:
            acc = pltpu.roll(acc, dx * 3 * CH, 1)
        result = jnp.where((lane >= dx * 3 * CH) & (lane < (dx + 1) * 3 * CH), acc, result)
    g = dot_t(gp_ref[CH : CH + R * CH, :], xb[...])
    g = jnp.concatenate([g, jnp.zeros((R * CH, 2 * S - g.shape[1]), F32)], axis=1)
    acc = g[0:CH, :]
    ones = g[0:CH, :]
    for r in range(1, R):
        part = g[r * CH : (r + 1) * CH, :]
        ones = ones + part
        acc = acc + pltpu.roll(part, 2 * S - r * FREQ, 1)
    acc = pltpu.roll(acc, 9 * CH, 1)
    ones = pltpu.roll(ones, 2 * S - 1 - 3 * XW, 1)
    result = jnp.where(lane >= 9 * CH, acc, result)
    w_ref[...] = jnp.where(lane == 2 * S - 1, ones, result)


def slots_kernel(rows_ref, gp_ref, big_ref, out_ref, grad, gsrc):
    oh_ref, mt_ref, t3_ref, _ = late(big_ref, out_ref.shape[0], 0)
    part = R * FREQ
    limit = rows_ref[0, 0]
    pad = 2 * FREQ
    grad[0:pad, :] = jnp.zeros((pad, S), F32)
    end = pad + S * FREQ
    grad[end:, :] = jnp.zeros((grad.shape[0] - end, S), F32)
    for n in range(0, LANES, 4 * S):
        u = dot(t3_ref[...], gp_ref[:, n : n + 4 * S])
        for b in range(4):
            m = n // S + b
            lanes = slice(b * S, (b + 1) * S)
            rows = shifted(u[0:part, lanes], 1) + u[part : 2 * part, lanes]
            rows = rows + shifted(u[2 * part : 3 * part, lanes], -1)
            y = (iota(rows.shape, 0) >> 2) + m * R
            grad[pad + m * part : pad + (m + 1) * part, :] = jnp.where(y < limit, rows, 0.0)
    step = 176
    for a in range(0, 3 * step, step):
        pair = jnp.concatenate(
            [grad[pad + a : pad + a + step, :], grad[FREQ + a : FREQ + a + step, :]], axis=1
        )
        gsrc[a : a + step, :] = dot(pair.astype(BF), mt_ref[...])
    gsrc[3 * step :, :] = jnp.zeros((gsrc.shape[0] - 3 * step, S), F32)
    for f in range(FREQ):
        rows = gsrc[pl.ds(f, SRC, stride=FREQ), :]
        high = rows.astype(BF)
        low = (rows - high.astype(F32)).astype(BF)
        out = dot(oh_ref[...], high) + dot(oh_ref[...], low)
        out_ref[:, f * S : (f + 1) * S] = out.astype(BF)


def pack_kernel(w_ref, buffer_ref, out_ref, packed, sems):
    del buffer_ref
    owners, chunk, _ = out_ref.shape
    total = w_ref[...]
    high = total.astype(BF)
    packed[:, 0 : 2 * S] = high
    packed[:, 2 * S : 4 * S] = (total - high.astype(F32)).astype(BF)
    copies = [
        pltpu.make_async_copy(packed, out_ref.at[t, pl.ds(chunk - CH, CH), :], sems.at[t])
        for t in range(owners)
    ]
    for copy in copies:
        copy.start()
    for copy in copies:
        copy.wait()


def final_kernel(scale, big_ref, back_ref, map_ref, w1_ref, bias_ref, w2_ref):
    blocks = map_ref.shape[0]
    sel_ref = late(big_ref, back_ref.shape[0], blocks)[-1]
    total = dot(sel_ref[...], back_ref[...])
    for f in range(FREQ):
        map_ref[:, f, :] = total[0:blocks, f * S : (f + 1) * S]
    weights = (total[blocks:, 0 : 2 * S] + total[blocks:, 2 * S : 4 * S]) * scale
    for dy in range(3):
        for dx in range(3):
            at = (dx * 3 + dy) * CH
            w2_ref[dy * 3 + dx] = weights[:, at : at + CH]
    flat = jnp.concatenate([weights[:, S:], jnp.zeros((S - CH, S), F32)], axis=0).T
    for dy in range(3):
        for dx in range(3):
            at = 9 * CH - S + dx * XW + dy * FREQ
            w1_ref[dy * 3 + dx] = flat[at : at + FREQ, 0:CH]
    bias_ref[...] = flat[S - 1 : S, 0:CH]


def vmem(n):
    return [pl.BlockSpec(memory_space=pltpu.VMEM)] * n


def hbm(n):
    return [pl.BlockSpec(memory_space=pl.ANY)] * n


def smem(n):
    return [pl.BlockSpec(memory_space=pltpu.SMEM)] * n


def call(kernel, out_shape, in_specs, out_specs, scratch=(), **extra):
    return pl.pallas_call(
        kernel,
        out_shape=out_shape,
        in_specs=in_specs,
        out_specs=out_specs,
        scratch_shapes=list(scratch),
        compiler_params=pltpu.CompilerParams(vmem_limit_bytes=VMEM_LIMIT),
        **extra,
    )


def arr(shape, dtype):
    return jax.ShapeDtypeStruct(shape, dtype)


def in_hbm(*values):
    return [pltpu.with_memory_space_constraint(value, pltpu.HBM) for value in values]


def in_vmem(*values):
    return [pltpu.with_memory_space_constraint(value, pltpu.VMEM) for value in values]


def band_sum(value, count, beside):
    if count & (count - 1):
        return lax.psum(value, "band"), beside
    step = 1
    while step < count:
        pairs = [(i, i ^ step) for i in range(count)]
        value = value + lax.ppermute(value, "band", pairs)
        if step == 1:
            value, beside = lax.optimization_barrier((value, beside))
        step *= 2
    return value, beside


def shards(
    pixel_map,
    interp_bands,
    conv1_weight,
    conv1_bias,
    conv2_weight,
    send_rows,
    patch_slots,
    patch_rows,
    cotangent,
):
    tile_count = lax.axis_size("tile")
    band_count = lax.axis_size("band")
    band_index = lax.axis_index("band")
    owned = pixel_map[0]
    blocks = owned.shape[0]
    send = send_rows[0, 0]
    capacity = send.shape[1]
    chunk = capacity + CH
    slots = patch_slots[0]
    cot = cotangent.reshape(CH * S, S)

    outgoing = call(
        outgoing_kernel,
        arr((tile_count * capacity, FREQ, S), BF),
        hbm(2),
        vmem(1)[0],
        (
            pltpu.SMEM(send.shape, I32),
            pltpu.VMEM(owned.shape, BF),
            pltpu.SemaphoreType.DMA((2,)),
        ),
    )(*in_hbm(send, owned))
    received = lax.all_to_all(outgoing, "tile", split_axis=0, concat_axis=0, tiled=True)

    is_polar = jnp.logical_or(
        band_index < band_count // 4, band_index >= band_count - band_count // 4
    )
    polar = is_polar.astype(I32).reshape(1)
    w1 = jnp.transpose(conv1_weight, (2, 3, 1, 0)).reshape(9, FREQ, CH)
    w2 = jnp.transpose(conv2_weight, (2, 3, 0, 1)).reshape(9, CH, CH)
    bias = conv1_bias.reshape(1, CH)
    cost = pl.CostEstimate(flops=4 * 10**9, bytes_accessed=4 * 10**6, transcendentals=0)
    big, gh = call(
        prepare_kernel,
        (pltpu.VMEM((3 * S, LANES + 3 * S), BF), pltpu.VMEM((R * CH, LANES), F32)),
        smem(1) + hbm(4),
        vmem(2),
        (
            pltpu.VMEM((3 * WIN, LANES), BF),
            pltpu.VMEM((CH * S, S), F32),
            pltpu.VMEM((R * CH, 3 * WIN), BF),
            pltpu.VMEM(cot.shape, BF),
            pltpu.VMEM(w1.shape, BF),
            pltpu.VMEM(w2.shape, BF),
            pltpu.VMEM(interp_bands.shape, BF),
            pltpu.VMEM((9 * FREQ, CH), F32),
            pltpu.VMEM((9 * CH, CH), F32),
            pltpu.SemaphoreType.DMA((4,)),
        ),
        cost_estimate=cost,
    )(polar, *in_hbm(cot, w1, w2, interp_bands))

    padded = (S + 4) * FREQ
    weights, gp = call(
        patch_kernel,
        (pltpu.VMEM((CH, 2 * S), F32), pltpu.VMEM((WIN, LANES), BF)),
        smem(2) + vmem(4),
        vmem(2),
        (
            pltpu.VMEM((padded + 8, S), F32),
            pltpu.VMEM((3, padded, S), BF),
            pltpu.VMEM((3 * XW + CH, LANES), BF),
            pltpu.VMEM((WIN, LANES), BF),
        ),
    )(slots, patch_rows, bias, received, *in_vmem(big, gh))

    rows = max(3 * S, tile_count * chunk)
    lists = call(
        functools.partial(lists_kernel, blocks),
        pltpu.VMEM((rows, 4 * S + tile_count * chunk), BF),
        smem(1) + hbm(5),
        vmem(1)[0],
        (
            pltpu.VMEM((1, tile_count * chunk), I32),
            pltpu.VMEM(w1.shape, BF),
            pltpu.VMEM(interp_bands.shape, BF),
            pltpu.VMEM(slots.shape, I32),
            pltpu.VMEM(send.shape, I32),
            pltpu.VMEM((9 * FREQ, CH), F32),
            pltpu.SemaphoreType.DMA((4,)),
        ),
        cost_estimate=cost,
    )(polar, *in_hbm(w1, interp_bands, slots, send), gp)
    weights, lists = band_sum(weights, band_count, lists)
    returning = call(
        slots_kernel,
        arr((tile_count * chunk, 4 * S), BF),
        smem(1) + vmem(2),
        vmem(1)[0],
        (pltpu.VMEM((padded + 16, S), F32), pltpu.VMEM((SRC * FREQ, S), F32)),
    )(patch_rows, *in_vmem(gp, lists))
    returning = call(
        pack_kernel,
        arr((tile_count, chunk, 4 * S), BF),
        vmem(1) + [pl.BlockSpec(memory_space=pl.ANY)],
        pl.BlockSpec(memory_space=pl.ANY),
        (pltpu.VMEM((CH, 4 * S), BF), pltpu.SemaphoreType.DMA((tile_count,))),
        input_output_aliases={1: 0},
    )(weights, returning.reshape(tile_count, chunk, 4 * S))
    returned = lax.all_to_all(returning, "tile", split_axis=0, concat_axis=0, tiled=True)
    norm_scale = float(band_count * tile_count * S * S) ** (-0.5)
    grad_map, grad1, grad_bias, grad2 = call(
        functools.partial(final_kernel, norm_scale),
        (
            arr((blocks, FREQ, S), F32),
            arr((9, FREQ, CH), F32),
            arr((1, CH), F32),
            arr((9, CH, CH), F32),
        ),
        vmem(2),
        vmem(4),
    )(*in_vmem(lists), returned.reshape(tile_count * chunk, 4 * S))
    return (
        grad_map[None],
        jnp.transpose(grad1.reshape(3, 3, FREQ, CH), (3, 2, 0, 1)),
        grad_bias.reshape(CH),
        jnp.transpose(grad2.reshape(3, 3, CH, CH), (2, 3, 0, 1)),
    )


def solution(mesh):
    in_specs = (
        P("band", "tile", None, None),
        P(),
        P(),
        P(),
        P(),
        P("band", "tile", None, None),
        P("band", "tile", None),
        P("band", "tile"),
        P("band", "tile", None, None, None),
    )
    out_specs = (P("band", "tile", None, None), P(), P(), P())
    return jax.shard_map(shards, mesh=mesh, in_specs=in_specs, out_specs=out_specs, check_vma=False)
```

```python
import functools

import jax
import jax.numpy as jnp
from jax import lax
from jax.experimental import pallas as pl
from jax.experimental.pallas import tpu as pltpu
from jax.sharding import PartitionSpec as P

BF = jnp.bfloat16
F32 = jnp.float32
I32 = jnp.int32
S = 128
FREQ = 4
CH = 16
R = 8
NB = S // R
WIN = (R + 2) * CH
XW = 48
LANES = NB * S
SRC = 144
VMEM_LIMIT = 16 * 1024 * 1024


def iota(shape, axis):
    return lax.broadcasted_iota(I32, shape, axis)


def dot(a, b):
    return lax.dot_general(a, b, (((1,), (0,)), ((), ())), preferred_element_type=F32)


def dot_t(a, b):
    return lax.dot_general(a, b, (((1,), (1,)), ((), ())), preferred_element_type=F32)


def shifted(rows, step):
    lane = iota(rows.shape, 1)
    if step == 1:
        return jnp.where(lane == S - 1, 0.0, pltpu.roll(rows, S - 1, 1))
    return jnp.where(lane == 0, 0.0, pltpu.roll(rows, 1, 1))


def store_window(ref, base, y, tile):
    block, r = divmod(y, R)
    ref[base + (r + 1) * CH : base + (r + 2) * CH, block * S : (block + 1) * S] = tile
    if r == 0 and block > 0:
        ref[base + (R + 1) * CH : base + WIN, (block - 1) * S : block * S] = tile
    if r == R - 1 and block < NB - 1:
        ref[base : base + CH, (block + 1) * S : (block + 2) * S] = tile


def zero_edges(ref, base):
    zero = jnp.zeros((CH, S), BF)
    ref[base : base + CH, 0:S] = zero
    ref[base + (R + 1) * CH : base + WIN, LANES - S : LANES] = zero


class View:
    def __init__(self, ref, row, rows, lane, lanes):
        self.ref, self.origin, self.shape = ref, (row, lane), (rows, lanes)

    def place(self, key):
        key = (slice(None), slice(None)) if key is Ellipsis else key
        spans = [k.indices(n) for k, n in zip(key, self.shape)]
        return tuple(slice(o + a, o + b) for o, (a, b, _) in zip(self.origin, spans))

    def __getitem__(self, key):
        return self.ref[self.place(key)]

    def __setitem__(self, key, value):
        self.ref[self.place(key)] = value


def early(ref):
    return View(ref, 2 * S, R * CH, LANES, 3 * XW + CH), View(ref, 0, 2 * S, LANES, 3 * S)


def late(ref, chunks, blocks):
    return (
        View(ref, 0, chunks, 0, SRC),
        View(ref, 0, 2 * S, 2 * S, S),
        View(ref, 2 * S, 3 * R * FREQ, 2 * S, WIN),
        View(ref, 0, blocks, 4 * S, chunks),
    )


def fetch(pairs, sems):
    copies = [pltpu.make_async_copy(a, b, sems.at[i]) for i, (a, b) in enumerate(pairs)]
    for copy in copies:
        copy.start()
    return copies


def outgoing_kernel(me_ref, send_hbm, map_hbm, *refs):
    out_refs, (rows_ref, map_ref, sems) = refs[:-3], refs[-3:]
    capacity = rows_ref.shape[1]
    for copy in fetch(((send_hbm, rows_ref), (map_hbm, map_ref)), sems):
        copy.wait()
    for j in range(2 * len(out_refs)):
        t = me_ref[0] ^ j
        for c in range(capacity):
            out_refs[j // 2][(j % 2) * capacity + c] = map_ref[rows_ref[t, c]]


def half_kernel(half, *refs):
    out_ref = refs[-1]
    capacity = refs[0].shape[0] // 2
    for d, ref in enumerate(refs[:-1]):
        out_ref[d * capacity : (d + 1) * capacity] = ref[half * capacity : (half + 1) * capacity]


def prepare_kernel(
    capacity,
    polar_ref,
    me_ref,
    cot_hbm,
    w1_hbm,
    w2_hbm,
    interp_hbm,
    slots_hbm,
    big_ref,
    gh_ref,
    picks_ref,
    slots_ref,
    cb_ref,
    plane,
    t2_ref,
    cot_ref,
    w1_ref,
    w2_ref,
    interp_ref,
    stack1,
    stack2,
    sems,
):
    copies = fetch(
        (
            (w1_hbm, w1_ref),
            (w2_hbm, w2_ref),
            (interp_hbm, interp_ref),
            (slots_hbm, slots_ref),
            (cot_hbm, cot_ref),
        ),
        sems,
    )
    t1_ref, ms_ref = early(big_ref)
    for copy in copies[:-1]:
        copy.wait()
    for i in range(9):
        stack1[i * FREQ : (i + 1) * FREQ, :] = w1_ref[i].astype(F32)
        stack2[i * CH : (i + 1) * CH, :] = w2_ref[i].astype(F32)
    pick = ((iota((R * CH, CH), 0) & 15) == iota((R * CH, CH), 1)).astype(BF)
    spread = dot_t(pick, stack2[...].astype(BF)).astype(BF)
    row, col = iota((R * CH, 3 * WIN), 0), iota((R * CH, 3 * WIN), 1)
    gap = ((col - jnp.where(col >= 2 * WIN, 2 * WIN, jnp.where(col >= WIN, WIN, 0))) >> 4) - (row >> 4)
    k, kcol = iota((CH * 9, 3 * WIN), 0), iota((CH * 9, 3 * WIN), 1)
    kdx = jnp.where(kcol >= 2 * WIN, 2, jnp.where(kcol >= WIN, 1, 0))
    source = kdx * CH + (kcol & 15)
    banded = jnp.zeros((R * CH, 3 * WIN), F32)
    for dy in range(3):
        term = dot(spread, (k == source + dy * 3 * CH).astype(BF))
        banded = jnp.where(gap == 2 - dy, term, banded)
    t2_ref[...] = banded.astype(BF)
    weights1 = stack1[...].astype(BF)
    spread = dot_t(pick, weights1).astype(BF)
    width = 3 * XW + CH
    row, col = iota((R * CH, width), 0), iota((R * CH, width), 1)
    cdx = jnp.where(col >= 3 * XW, 3, jnp.where(col >= 2 * XW, 2, jnp.where(col >= XW, 1, 0)))
    gap = ((col - cdx * XW) >> 2) - (row >> 4)
    gap = jnp.where(cdx == 3, -1, gap)
    k, kcol = iota((FREQ * 9, width), 0), iota((FREQ * 9, width), 1)
    kdx = jnp.where(kcol >= 3 * XW, 3, jnp.where(kcol >= 2 * XW, 2, jnp.where(kcol >= XW, 1, 0)))
    source = kdx * FREQ + (kcol & 3)
    banded = jnp.zeros((R * CH, width), F32)
    for dy in range(3):
        term = dot(spread, (k == source + dy * 3 * FREQ).astype(BF))
        banded = jnp.where(gap == dy, term, banded)
    t1_ref[...] = banded.astype(BF)

    for half in range(2):
        matrix = jnp.where(
            polar_ref[0] == 1, interp_ref[0, half].astype(F32), interp_ref[1, half].astype(F32)
        )
        at = slice(half * S, (half + 1) * S)
        ms_ref[at, 0:S] = shifted(matrix, -1).astype(BF)
        ms_ref[at, S : 2 * S] = matrix.astype(BF)
        ms_ref[at, 2 * S : 3 * S] = shifted(matrix, 1).astype(BF)

    half = picks_ref.shape[1] // 2
    for k in range(slots_ref.shape[1]):
        slot = slots_ref[0, k]
        owner = lax.div(slot, capacity)
        j = owner ^ me_ref[0]
        picks_ref[0, k] = j & 1
        picks_ref[0, half + k] = (j >> 1) * capacity + slot - owner * capacity

    copies[-1].wait()
    for o in range(CH):
        plane[o * S : (o + 1) * S, :] = cot_ref[o * S : (o + 1) * S, :].astype(F32)
    for dx in range(3):
        zero_edges(cb_ref, dx * WIN)
    for y in range(S):
        rows = plane[pl.ds(y, CH, stride=S), :]
        block, r = divmod(y, R)
        for dx, tile in enumerate((shifted(rows, 1), rows, shifted(rows, -1))):
            tile = tile.astype(BF)
            store_window(cb_ref, dx * WIN, y, tile)
            at = dx * S + r * CH
            big_ref[at : at + CH, block * S : (block + 1) * S] = tile
    for n in range(0, LANES, 512):
        gh_ref[:, n : n + 512] = dot(t2_ref[...], cb_ref[:, n : n + 512])


def lists_kernel(
    blocks,
    polar_ref,
    me_ref,
    w1_hbm,
    interp_hbm,
    slots_hbm,
    send_hbm,
    after_hbm,
    big_ref,
    lists,
    w1_ref,
    interp_ref,
    slots_ref,
    send_ref,
    stack1,
    sems,
):
    del after_hbm
    pairs = (
        (w1_hbm, w1_ref),
        (interp_hbm, interp_ref),
        (slots_hbm, slots_ref),
        (send_hbm, send_ref),
    )
    for copy in fetch(pairs, sems):
        copy.wait()
    owners, capacity = send_ref.shape
    nsrc = slots_ref.shape[1]
    oh_ref, mt_ref, t3_ref, sel_ref = late(big_ref, owners * capacity, blocks)
    for i in range(9):
        stack1[i * FREQ : (i + 1) * FREQ, :] = w1_ref[i].astype(F32)
    weights1 = stack1[...].astype(BF)
    part = R * FREQ
    tall = 3 * part
    row, k = iota((tall, FREQ * 9), 0), iota((tall, FREQ * 9), 1)
    rdx = jnp.where(row >= 2 * part, 2, jnp.where(row >= part, 1, 0))
    source = rdx * FREQ + (row & 3)
    column = ((iota((CH, WIN), 1) & 15) == iota((CH, WIN), 0)).astype(BF)
    row, col = iota((tall, WIN), 0), iota((tall, WIN), 1)
    gap = (col >> 4) - ((row & (part - 1)) >> 2)
    banded = jnp.zeros((tall, WIN), F32)
    for dy in range(3):
        spread = dot((k == source + dy * 3 * FREQ).astype(BF), weights1).astype(BF)
        banded = jnp.where(gap == 2 - dy, dot(spread, column), banded)
    t3_ref[...] = banded.astype(BF)

    for half in range(2):
        matrix = jnp.where(
            polar_ref[0] == 1, interp_ref[0, half].astype(F32), interp_ref[1, half].astype(F32)
        )
        mt_ref[half * S : (half + 1) * S, :] = matrix.T.astype(BF)

    slots = jnp.concatenate([slots_ref[...], jnp.full((1, SRC - nsrc), -1, I32)], axis=1)
    for j in range(owners):
        t = me_ref[0] ^ j
        c = iota((capacity, SRC), 0)
        hit = jnp.where(c + t * capacity == slots, 1.0, 0.0)
        oh_ref[j * capacity : (j + 1) * capacity, :] = hit.astype(BF)
        at = ((j % 2) * (owners // 2) + j // 2) * capacity
        lists[0:1, at : at + capacity] = send_ref[pl.ds(t, 1), :]
    hit = lists[...] == iota(sel_ref.shape, 0)
    sel_ref[...] = jnp.where(hit, 1.0, 0.0).astype(BF)


def patch_kernel(
    nsrc,
    picks_ref,
    rows_ref,
    bias_ref,
    near_ref,
    far_ref,
    big_ref,
    gh_ref,
    w_ref,
    gp_ref,
    src,
    img,
    xb,
    hb,
):
    half = picks_ref.shape[1] // 2
    total = src.shape[0]
    t1_ref, ms_ref = early(big_ref)
    src[0:FREQ, :] = jnp.zeros((FREQ, S), F32)
    first = FREQ * (nsrc + 1)
    src[first:total, :] = jnp.zeros((total - first, S), F32)
    for k in range(nsrc):
        at = picks_ref[0, half + k]
        block = jnp.where(picks_ref[0, k] == 0, near_ref[at].astype(F32), far_ref[at].astype(F32))
        src[FREQ * (k + 1) : FREQ * (k + 2), :] = block
    limit = FREQ * (rows_ref[0, 0] + 1)
    step = img.shape[1] // 3
    for a in range(0, img.shape[1], step):
        pair = jnp.concatenate([src[a : a + step, :], src[a + FREQ : a + FREQ + step, :]], axis=1)
        out = dot(pair.astype(BF), ms_ref[...])
        at = iota(out.shape, 0) + a
        out = jnp.where((at >= FREQ) & (at < limit), out, 0.0).astype(BF)
        for dx in range(3):
            img[dx, a : a + step, :] = out[:, dx * S : (dx + 1) * S]
    for m in range(NB):
        for dx in range(3):
            xb[dx * XW : (dx + 1) * XW, m * S : (m + 1) * S] = img[
                dx, m * R * FREQ : m * R * FREQ + XW, :
            ]
    xb[3 * XW :, :] = jnp.ones((CH, LANES), BF)
    zero_edges(hb, 0)
    zero_edges(gp_ref, 0)
    own = (iota((R * CH, CH), 0) & 15) == iota((R * CH, CH), 1)
    bias = jnp.sum(jnp.where(own, bias_ref[...], 0.0), axis=1, keepdims=True)
    for n in range(0, LANES, 2 * S):
        pre = dot(t1_ref[...], xb[:, n : n + 2 * S]) + bias
        gate = jax.nn.sigmoid(pre)
        hidden = (pre * gate).astype(BF)
        grad = (gh_ref[:, n : n + 2 * S] * (gate * (1.0 + pre * (1.0 - gate)))).astype(BF)
        for b in range(2):
            m = n // S + b
            lanes = slice(b * S, (b + 1) * S)
            for ref, value in ((hb, hidden), (gp_ref, grad)):
                ref[CH : CH + R * CH, m * S : (m + 1) * S] = value[:, lanes]
                if m > 0:
                    ref[(R + 1) * CH : WIN, (m - 1) * S : m * S] = value[0:CH, lanes]
                if m < NB - 1:
                    ref[0:CH, (m + 1) * S : (m + 2) * S] = value[(R - 1) * CH :, lanes]
    lane = iota((CH, 2 * S), 1)
    result = jnp.zeros((CH, 2 * S), F32)
    for dx in range(3):
        g = dot_t(big_ref[dx * S : (dx + 1) * S, 0:LANES], hb[...])
        g = jnp.concatenate([g, jnp.zeros((R * CH, 2 * S - WIN), F32)], axis=1)
        acc = g[0:CH, :]
        for r in range(1, R):
            acc = acc + pltpu.roll(g[r * CH : (r + 1) * CH, :], 2 * S - r * CH, 1)
        if dx:
            acc = pltpu.roll(acc, dx * 3 * CH, 1)
        result = jnp.where((lane >= dx * 3 * CH) & (lane < (dx + 1) * 3 * CH), acc, result)
    g = dot_t(gp_ref[CH : CH + R * CH, :], xb[...])
    g = jnp.concatenate([g, jnp.zeros((R * CH, 2 * S - g.shape[1]), F32)], axis=1)
    acc = g[0:CH, :]
    ones = g[0:CH, :]
    for r in range(1, R):
        part = g[r * CH : (r + 1) * CH, :]
        ones = ones + part
        acc = acc + pltpu.roll(part, 2 * S - r * FREQ, 1)
    acc = pltpu.roll(acc, 9 * CH, 1)
    ones = pltpu.roll(ones, 2 * S - 1 - 3 * XW, 1)
    result = jnp.where(lane >= 9 * CH, acc, result)
    w_ref[...] = jnp.where(lane == 2 * S - 1, ones, result)


def slots_kernel(rows_ref, gp_ref, big_ref, *refs):
    out_refs, (grad, gsrc) = refs[:-2], refs[-2:]
    height = out_refs[0].shape[0]
    oh_ref, mt_ref, t3_ref, _ = late(big_ref, height * len(out_refs), 0)
    part = R * FREQ
    limit = rows_ref[0, 0]
    pad = 2 * FREQ
    grad[0:pad, :] = jnp.zeros((pad, S), F32)
    end = pad + S * FREQ
    grad[end:, :] = jnp.zeros((grad.shape[0] - end, S), F32)
    for n in range(0, LANES, 4 * S):
        u = dot(t3_ref[...], gp_ref[:, n : n + 4 * S])
        for b in range(4):
            m = n // S + b
            lanes = slice(b * S, (b + 1) * S)
            rows = shifted(u[0:part, lanes], 1) + u[part : 2 * part, lanes]
            rows = rows + shifted(u[2 * part : 3 * part, lanes], -1)
            y = (iota(rows.shape, 0) >> 2) + m * R
            grad[pad + m * part : pad + (m + 1) * part, :] = jnp.where(y < limit, rows, 0.0)
    step = 176
    for a in range(0, 3 * step, step):
        pair = jnp.concatenate(
            [grad[pad + a : pad + a + step, :], grad[FREQ + a : FREQ + a + step, :]], axis=1
        )
        gsrc[a : a + step, :] = dot(pair.astype(BF), mt_ref[...])
    gsrc[3 * step :, :] = jnp.zeros((gsrc.shape[0] - 3 * step, S), F32)
    for f in range(FREQ):
        rows = gsrc[pl.ds(f, SRC, stride=FREQ), :]
        high = rows.astype(BF)
        low = (rows - high.astype(F32)).astype(BF)
        out = dot(oh_ref[...], high) + dot(oh_ref[...], low)
        for d, out_ref in enumerate(out_refs):
            rows = out[d * height : (d + 1) * height, :]
            out_ref[0:height, f * S : (f + 1) * S] = rows.astype(BF)


def split(value):
    high = value.astype(BF)
    return high, (value - high.astype(F32)).astype(BF)


def joined(rows):
    return rows[:, 0 : 2 * S].astype(F32) + rows[:, 2 * S : 4 * S].astype(F32)


def pack_kernel(w_ref, *refs):
    count = (len(refs) - 2) // 2
    out_refs, (packed, sems) = refs[count:-2], refs[-2:]
    packed[:, 0 : 2 * S], packed[:, 2 * S : 4 * S] = split(w_ref[...])
    pairs = [(packed, ref.at[pl.ds(ref.shape[0] - CH, CH), :]) for ref in out_refs]
    for copy in fetch(pairs, sems):
        copy.wait()


def relay_kernel(w_ref, own_ref, *refs):
    in_refs, (out_ref, sum_ref) = refs[:-2], refs[-2:]
    pair = own_ref.shape[0]
    capacity = pair // 2
    total = w_ref[...]
    for d, ref in enumerate((own_ref, *in_refs)):
        out_ref[d * capacity : (d + 1) * capacity, :] = ref[capacity:pair, :]
        if d:
            total = total + joined(ref[pair : pair + CH, :])
    sum_ref[...] = total
    at = out_ref.shape[0] - CH
    out_ref[at:, 0 : 2 * S], out_ref[at:, 2 * S : 4 * S] = split(total)


def final_kernel(scale, big_ref, sum_ref, *refs):
    in_refs, far_ref, (map_ref, w1_ref, bias_ref, w2_ref) = refs[:-5], refs[-5], refs[-4:]
    blocks = map_ref.shape[0]
    capacity = in_refs[0].shape[0] // 2
    middle = capacity * len(in_refs)
    sel = late(big_ref, 2 * middle, blocks)[-1][...]
    near = jnp.concatenate([ref[0:capacity, :] for ref in in_refs], axis=0)
    total = dot(sel, jnp.concatenate([near, far_ref[0:middle, :]], axis=0))
    for f in range(FREQ):
        map_ref[:, f, :] = total[:, f * S : (f + 1) * S]
    weights = (sum_ref[...] + joined(far_ref[middle:, :])) * scale
    for dy in range(3):
        for dx in range(3):
            at = (dx * 3 + dy) * CH
            w2_ref[dy * 3 + dx] = weights[:, at : at + CH]
    flat = jnp.concatenate([weights[:, S:], jnp.zeros((S - CH, S), F32)], axis=0).T
    for dy in range(3):
        for dx in range(3):
            at = 9 * CH - S + dx * XW + dy * FREQ
            w1_ref[dy * 3 + dx] = flat[at : at + FREQ, 0:CH]
    bias_ref[...] = flat[S - 1 : S, 0:CH]


def vmem(n):
    return [pl.BlockSpec(memory_space=pltpu.VMEM)] * n


def hbm(n):
    return [pl.BlockSpec(memory_space=pl.ANY)] * n


def smem(n):
    return [pl.BlockSpec(memory_space=pltpu.SMEM)] * n


def call(kernel, out_shape, in_specs, out_specs, scratch=(), **extra):
    return pl.pallas_call(
        kernel,
        out_shape=out_shape,
        in_specs=in_specs,
        out_specs=out_specs,
        scratch_shapes=list(scratch),
        compiler_params=pltpu.CompilerParams(vmem_limit_bytes=VMEM_LIMIT),
        **extra,
    )


def arr(shape, dtype):
    return jax.ShapeDtypeStruct(shape, dtype)


def in_hbm(*values):
    return [pltpu.with_memory_space_constraint(value, pltpu.HBM) for value in values]


def in_vmem(*values):
    return [pltpu.with_memory_space_constraint(value, pltpu.VMEM) for value in values]


def band_sum(value, count, beside):
    if count & (count - 1):
        return lax.psum(value, "band"), beside
    step = 1
    while step < count:
        pairs = [(i, i ^ step) for i in range(count)]
        value = value + lax.ppermute(value, "band", pairs)
        if step == 1:
            value, beside = lax.optimization_barrier((value, beside))
        step *= 2
    return value, beside


def to_chips(values, count):
    return [
        lax.ppermute(value, "tile", [(i, i ^ (2 * d)) for i in range(count)])
        for d, value in enumerate(values, 1)
    ]


def to_core(value, count):
    return lax.ppermute(value, "tile", [(i, i ^ 1) for i in range(count)])


def shards(
    pixel_map,
    interp_bands,
    conv1_weight,
    conv1_bias,
    conv2_weight,
    send_rows,
    patch_slots,
    patch_rows,
    cotangent,
):
    tile_count = lax.axis_size("tile")
    band_count = lax.axis_size("band")
    band_index = lax.axis_index("band")
    owned = pixel_map[0]
    blocks = owned.shape[0]
    send = send_rows[0, 0]
    capacity = send.shape[1]
    chips = tile_count // 2
    slots = patch_slots[0]
    cot = cotangent.reshape(CH * S, S)

    me = lax.axis_index("tile").astype(I32).reshape(1)
    outgoing = call(
        outgoing_kernel,
        [arr((2 * capacity, FREQ, S), BF)] * chips,
        smem(1) + hbm(2),
        vmem(chips),
        (
            pltpu.SMEM(send.shape, I32),
            pltpu.VMEM(owned.shape, BF),
            pltpu.SemaphoreType.DMA((2,)),
        ),
    )(me, *in_hbm(send, owned))
    received = [outgoing[0]] + to_chips(outgoing[1:], tile_count)
    is_polar = jnp.logical_or(
        band_index < band_count // 4, band_index >= band_count - band_count // 4
    )
    polar = is_polar.astype(I32).reshape(1)
    w1 = jnp.transpose(conv1_weight, (2, 3, 1, 0)).reshape(9, FREQ, CH)
    w2 = jnp.transpose(conv2_weight, (2, 3, 0, 1)).reshape(9, CH, CH)
    bias = conv1_bias.reshape(1, CH)
    cost = pl.CostEstimate(flops=4 * 10**9, bytes_accessed=4 * 10**6, transcendentals=0)
    big, gh, picks = call(
        functools.partial(prepare_kernel, capacity),
        (
            pltpu.VMEM((3 * S, LANES + 3 * S), BF),
            pltpu.VMEM((R * CH, LANES), F32),
            pltpu.SMEM((1, 2 * SRC), I32),
        ),
        smem(2) + hbm(5),
        vmem(2) + smem(1),
        (
            pltpu.SMEM(slots.shape, I32),
            pltpu.VMEM((3 * WIN, LANES), BF),
            pltpu.VMEM((CH * S, S), F32),
            pltpu.VMEM((R * CH, 3 * WIN), BF),
            pltpu.VMEM(cot.shape, BF),
            pltpu.VMEM(w1.shape, BF),
            pltpu.VMEM(w2.shape, BF),
            pltpu.VMEM(interp_bands.shape, BF),
            pltpu.VMEM((9 * FREQ, CH), F32),
            pltpu.VMEM((9 * CH, CH), F32),
            pltpu.SemaphoreType.DMA((5,)),
        ),
        cost_estimate=cost,
    )(polar, me, *in_hbm(cot, w1, w2, interp_bands, slots))

    big, *received = lax.optimization_barrier((big, *received))
    blocks_half = pltpu.VMEM((chips * capacity, FREQ, S), BF)
    relayed = call(functools.partial(half_kernel, 1), blocks_half, vmem(chips), vmem(1)[0])(*received)
    far = to_core(relayed, tile_count)
    near = call(functools.partial(half_kernel, 0), blocks_half, vmem(chips), vmem(1)[0])(*received)

    padded = (S + 4) * FREQ
    weights, gp = call(
        functools.partial(patch_kernel, slots.shape[1]),
        (pltpu.VMEM((CH, 2 * S), F32), pltpu.VMEM((WIN, LANES), BF)),
        smem(2) + vmem(5),
        vmem(2),
        (
            pltpu.VMEM((padded + 8, S), F32),
            pltpu.VMEM((3, padded, S), BF),
            pltpu.VMEM((3 * XW + CH, LANES), BF),
            pltpu.VMEM((WIN, LANES), BF),
        ),
    )(picks, patch_rows, bias, near, far, *in_vmem(big, gh))

    rows = max(3 * S, tile_count * capacity)
    lists = call(
        functools.partial(lists_kernel, blocks),
        pltpu.VMEM((rows, 4 * S + tile_count * capacity), BF),
        smem(2) + hbm(5),
        vmem(1)[0],
        (
            pltpu.VMEM((1, tile_count * capacity), I32),
            pltpu.VMEM(w1.shape, BF),
            pltpu.VMEM(interp_bands.shape, BF),
            pltpu.VMEM(slots.shape, I32),
            pltpu.VMEM(send.shape, I32),
            pltpu.VMEM((9 * FREQ, CH), F32),
            pltpu.SemaphoreType.DMA((4,)),
        ),
        cost_estimate=cost,
    )(polar, me, *in_hbm(w1, interp_bands, slots, send), gp)
    weights, lists = band_sum(weights, band_count, lists)
    pair = 2 * capacity
    full = arr((pair + CH, 4 * S), BF)
    returning = call(
        slots_kernel,
        [arr((pair, 4 * S), BF)] + [full] * (chips - 1),
        smem(1) + vmem(2),
        vmem(chips),
        (pltpu.VMEM((padded + 16, S), F32), pltpu.VMEM((SRC * FREQ, S), F32)),
    )(patch_rows, *in_vmem(gp, lists))
    own = returning[0]
    packed = call(
        pack_kernel,
        [full] * (chips - 1),
        vmem(1) + hbm(chips - 1),
        hbm(chips - 1),
        (pltpu.VMEM((CH, 4 * S), BF), pltpu.SemaphoreType.DMA((chips - 1,))),
        input_output_aliases={i: i - 1 for i in range(1, chips)},
    )(weights, *returning[1:])
    returned = to_chips(packed, tile_count)
    relayed, total = call(
        relay_kernel,
        (arr((chips * capacity + CH, 4 * S), BF), arr((CH, 2 * S), F32)),
        vmem(1 + chips),
        vmem(2),
    )(weights, own, *returned)
    back = to_core(relayed, tile_count)
    norm_scale = float(band_count * tile_count * S * S) ** (-0.5)
    grad_map, grad1, grad_bias, grad2 = call(
        functools.partial(final_kernel, norm_scale),
        (
            arr((blocks, FREQ, S), F32),
            arr((9, FREQ, CH), F32),
            arr((1, CH), F32),
            arr((9, CH, CH), F32),
        ),
        vmem(3 + chips),
        vmem(4),
    )(*in_vmem(lists), total, own, *returned, back)
    return (
        grad_map[None],
        jnp.transpose(grad1.reshape(3, 3, FREQ, CH), (3, 2, 0, 1)),
        grad_bias.reshape(CH),
        jnp.transpose(grad2.reshape(3, 3, CH, CH), (2, 3, 0, 1)),
    )


def solution(mesh):
    in_specs = (
        P("band", "tile", None, None),
        P(),
        P(),
        P(),
        P(),
        P("band", "tile", None, None),
        P("band", "tile", None),
        P("band", "tile"),
        P("band", "tile", None, None, None),
    )
    out_specs = (P("band", "tile", None, None), P(), P(), P())
    return jax.shard_map(shards, mesh=mesh, in_specs=in_specs, out_specs=out_specs, check_vma=False)
```

```python
import functools

import jax
import jax.numpy as jnp
from jax import lax
from jax.experimental import pallas as pl
from jax.experimental.pallas import tpu as pltpu
from jax.sharding import PartitionSpec as P

BF = jnp.bfloat16
F32 = jnp.float32
I32 = jnp.int32
S = 128
FREQ = 4
CH = 16
R = 8
NB = S // R
WIN = (R + 2) * CH
XW = 48
LANES = NB * S
SRC = 144
VMEM_LIMIT = 16 * 1024 * 1024


def iota(shape, axis):
    return lax.broadcasted_iota(I32, shape, axis)


def dot(a, b):
    return lax.dot_general(a, b, (((1,), (0,)), ((), ())), preferred_element_type=F32)


def dot_t(a, b):
    return lax.dot_general(a, b, (((1,), (1,)), ((), ())), preferred_element_type=F32)


def shifted(rows, step):
    lane = iota(rows.shape, 1)
    if step == 1:
        return jnp.where(lane == S - 1, 0.0, pltpu.roll(rows, S - 1, 1))
    return jnp.where(lane == 0, 0.0, pltpu.roll(rows, 1, 1))


def store_window(ref, base, y, tile):
    block, r = divmod(y, R)
    ref[base + (r + 1) * CH : base + (r + 2) * CH, block * S : (block + 1) * S] = tile
    if r == 0 and block > 0:
        ref[base + (R + 1) * CH : base + WIN, (block - 1) * S : block * S] = tile
    if r == R - 1 and block < NB - 1:
        ref[base : base + CH, (block + 1) * S : (block + 2) * S] = tile


def zero_edges(ref, base):
    zero = jnp.zeros((CH, S), BF)
    ref[base : base + CH, 0:S] = zero
    ref[base + (R + 1) * CH : base + WIN, LANES - S : LANES] = zero


class View:
    def __init__(self, ref, row, rows, lane, lanes):
        self.ref, self.origin, self.shape = ref, (row, lane), (rows, lanes)

    def place(self, key):
        key = (slice(None), slice(None)) if key is Ellipsis else key
        spans = [k.indices(n) for k, n in zip(key, self.shape)]
        return tuple(slice(o + a, o + b) for o, (a, b, _) in zip(self.origin, spans))

    def __getitem__(self, key):
        return self.ref[self.place(key)]

    def __setitem__(self, key, value):
        self.ref[self.place(key)] = value


def early(ref):
    return View(ref, 2 * S, R * CH, LANES, 3 * XW + CH), View(ref, 0, 2 * S, LANES, 3 * S)


def late(ref, chunks, blocks):
    return (
        View(ref, 0, chunks, 0, SRC),
        View(ref, 0, 2 * S, 2 * S, S),
        View(ref, 2 * S, 3 * R * FREQ, 2 * S, WIN),
        View(ref, 0, blocks, 4 * S, chunks),
    )


def spot(d, chips):
    return -d & (chips - 1)


def fetch(pairs, sems):
    copies = [pltpu.make_async_copy(a, b, sems.at[i]) for i, (a, b) in enumerate(pairs)]
    for copy in copies:
        copy.start()
    return copies


def outgoing_kernel(me_ref, send_hbm, map_hbm, *refs):
    out_refs, (rows_ref, map_ref, sems) = refs[:-3], refs[-3:]
    capacity = rows_ref.shape[1]
    for copy in fetch(((send_hbm, rows_ref), (map_hbm, map_ref)), sems):
        copy.wait()
    chips = len(out_refs)
    for j in range(2 * chips):
        t = me_ref[0] ^ j
        for c in range(capacity):
            out_refs[spot(j // 2, chips)][(j % 2) * capacity + c] = map_ref[rows_ref[t, c]]


def half_kernel(half, *refs):
    out_ref = refs[-1]
    capacity = refs[0].shape[0] // 2
    for d, ref in enumerate(refs[:-1]):
        out_ref[d * capacity : (d + 1) * capacity] = ref[half * capacity : (half + 1) * capacity]


def prepare_kernel(
    chips,
    capacity,
    polar_ref,
    me_ref,
    cot_hbm,
    w1_hbm,
    w2_hbm,
    interp_hbm,
    slots_hbm,
    big_ref,
    gh_ref,
    picks_ref,
    slots_ref,
    cb_ref,
    plane,
    t2_ref,
    cot_ref,
    w1_ref,
    w2_ref,
    interp_ref,
    stack1,
    stack2,
    sems,
):
    copies = fetch(
        (
            (w1_hbm, w1_ref),
            (w2_hbm, w2_ref),
            (interp_hbm, interp_ref),
            (slots_hbm, slots_ref),
            (cot_hbm, cot_ref),
        ),
        sems,
    )
    t1_ref, ms_ref = early(big_ref)
    for copy in copies[:-1]:
        copy.wait()
    for i in range(9):
        stack1[i * FREQ : (i + 1) * FREQ, :] = w1_ref[i].astype(F32)
        stack2[i * CH : (i + 1) * CH, :] = w2_ref[i].astype(F32)
    pick = ((iota((R * CH, CH), 0) & 15) == iota((R * CH, CH), 1)).astype(BF)
    spread = dot_t(pick, stack2[...].astype(BF)).astype(BF)
    row, col = iota((R * CH, 3 * WIN), 0), iota((R * CH, 3 * WIN), 1)
    gap = ((col - jnp.where(col >= 2 * WIN, 2 * WIN, jnp.where(col >= WIN, WIN, 0))) >> 4) - (row >> 4)
    k, kcol = iota((CH * 9, 3 * WIN), 0), iota((CH * 9, 3 * WIN), 1)
    kdx = jnp.where(kcol >= 2 * WIN, 2, jnp.where(kcol >= WIN, 1, 0))
    source = kdx * CH + (kcol & 15)
    banded = jnp.zeros((R * CH, 3 * WIN), F32)
    for dy in range(3):
        term = dot(spread, (k == source + dy * 3 * CH).astype(BF))
        banded = jnp.where(gap == 2 - dy, term, banded)
    t2_ref[...] = banded.astype(BF)
    weights1 = stack1[...].astype(BF)
    spread = dot_t(pick, weights1).astype(BF)
    width = 3 * XW + CH
    row, col = iota((R * CH, width), 0), iota((R * CH, width), 1)
    cdx = jnp.where(col >= 3 * XW, 3, jnp.where(col >= 2 * XW, 2, jnp.where(col >= XW, 1, 0)))
    gap = ((col - cdx * XW) >> 2) - (row >> 4)
    gap = jnp.where(cdx == 3, -1, gap)
    k, kcol = iota((FREQ * 9, width), 0), iota((FREQ * 9, width), 1)
    kdx = jnp.where(kcol >= 3 * XW, 3, jnp.where(kcol >= 2 * XW, 2, jnp.where(kcol >= XW, 1, 0)))
    source = kdx * FREQ + (kcol & 3)
    banded = jnp.zeros((R * CH, width), F32)
    for dy in range(3):
        term = dot(spread, (k == source + dy * 3 * FREQ).astype(BF))
        banded = jnp.where(gap == dy, term, banded)
    t1_ref[...] = banded.astype(BF)

    for half in range(2):
        matrix = jnp.where(
            polar_ref[0] == 1, interp_ref[0, half].astype(F32), interp_ref[1, half].astype(F32)
        )
        at = slice(half * S, (half + 1) * S)
        ms_ref[at, 0:S] = shifted(matrix, -1).astype(BF)
        ms_ref[at, S : 2 * S] = matrix.astype(BF)
        ms_ref[at, 2 * S : 3 * S] = shifted(matrix, 1).astype(BF)

    half = picks_ref.shape[1] // 2
    for k in range(slots_ref.shape[1]):
        slot = slots_ref[0, k]
        if capacity & (capacity - 1):
            owner = lax.div(slot, capacity)
        else:
            owner = slot >> (capacity.bit_length() - 1)
        j = owner ^ me_ref[0]
        picks_ref[0, k] = j & 1
        picks_ref[0, half + k] = (spot(j >> 1, chips) - owner) * capacity + slot

    copies[-1].wait()
    for o in range(CH):
        plane[o * S : (o + 1) * S, :] = cot_ref[o * S : (o + 1) * S, :].astype(F32)
    for dx in range(3):
        zero_edges(cb_ref, dx * WIN)
    for y in range(S):
        rows = plane[pl.ds(y, CH, stride=S), :]
        block, r = divmod(y, R)
        for dx, tile in enumerate((shifted(rows, 1), rows, shifted(rows, -1))):
            tile = tile.astype(BF)
            store_window(cb_ref, dx * WIN, y, tile)
            at = dx * S + r * CH
            big_ref[at : at + CH, block * S : (block + 1) * S] = tile
    for n in range(0, LANES, 512):
        gh_ref[:, n : n + 512] = dot(t2_ref[...], cb_ref[:, n : n + 512])


def lists_kernel(
    blocks,
    polar_ref,
    me_ref,
    w1_hbm,
    interp_hbm,
    slots_hbm,
    send_hbm,
    after_hbm,
    big_ref,
    lists,
    w1_ref,
    interp_ref,
    slots_ref,
    send_ref,
    stack1,
    sems,
):
    del after_hbm
    pairs = (
        (w1_hbm, w1_ref),
        (interp_hbm, interp_ref),
        (slots_hbm, slots_ref),
        (send_hbm, send_ref),
    )
    for copy in fetch(pairs, sems):
        copy.wait()
    owners, capacity = send_ref.shape
    nsrc = slots_ref.shape[1]
    oh_ref, mt_ref, t3_ref, sel_ref = late(big_ref, owners * capacity, blocks)
    for i in range(9):
        stack1[i * FREQ : (i + 1) * FREQ, :] = w1_ref[i].astype(F32)
    weights1 = stack1[...].astype(BF)
    part = R * FREQ
    tall = 3 * part
    row, k = iota((tall, FREQ * 9), 0), iota((tall, FREQ * 9), 1)
    rdx = jnp.where(row >= 2 * part, 2, jnp.where(row >= part, 1, 0))
    source = rdx * FREQ + (row & 3)
    column = ((iota((CH, WIN), 1) & 15) == iota((CH, WIN), 0)).astype(BF)
    row, col = iota((tall, WIN), 0), iota((tall, WIN), 1)
    gap = (col >> 4) - ((row & (part - 1)) >> 2)
    banded = jnp.zeros((tall, WIN), F32)
    for dy in range(3):
        spread = dot((k == source + dy * 3 * FREQ).astype(BF), weights1).astype(BF)
        banded = jnp.where(gap == 2 - dy, dot(spread, column), banded)
    t3_ref[...] = banded.astype(BF)

    for half in range(2):
        matrix = jnp.where(
            polar_ref[0] == 1, interp_ref[0, half].astype(F32), interp_ref[1, half].astype(F32)
        )
        mt_ref[half * S : (half + 1) * S, :] = matrix.T.astype(BF)

    slots = jnp.concatenate([slots_ref[...], jnp.full((1, SRC - nsrc), -1, I32)], axis=1)
    for j in range(owners):
        t = me_ref[0] ^ j
        c = iota((capacity, SRC), 0)
        hit = jnp.where(c + t * capacity == slots, 1.0, 0.0)
        place = spot(j // 2, owners // 2)
        at = (2 * place + j % 2) * capacity
        oh_ref[at : at + capacity, :] = hit.astype(BF)
        at = ((j % 2) * (owners // 2) + place) * capacity
        lists[0:1, at : at + capacity] = send_ref[pl.ds(t, 1), :]
    hit = lists[...] == iota(sel_ref.shape, 0)
    sel_ref[...] = jnp.where(hit, 1.0, 0.0).astype(BF)


def patch_kernel(
    nsrc,
    picks_ref,
    rows_ref,
    bias_ref,
    near_ref,
    far_ref,
    big_ref,
    gh_ref,
    w_ref,
    gp_ref,
    src,
    img,
    xb,
    hb,
):
    half = picks_ref.shape[1] // 2
    total = src.shape[0]
    t1_ref, ms_ref = early(big_ref)
    src[0:FREQ, :] = jnp.zeros((FREQ, S), F32)
    first = FREQ * (nsrc + 1)
    src[first:total, :] = jnp.zeros((total - first, S), F32)
    for k in range(nsrc):
        at = picks_ref[0, half + k]
        block = jnp.where(picks_ref[0, k] == 0, near_ref[at].astype(F32), far_ref[at].astype(F32))
        src[FREQ * (k + 1) : FREQ * (k + 2), :] = block
    limit = FREQ * (rows_ref[0, 0] + 1)
    step = img.shape[1] // 3
    for a in range(0, img.shape[1], step):
        pair = jnp.concatenate([src[a : a + step, :], src[a + FREQ : a + FREQ + step, :]], axis=1)
        out = dot(pair.astype(BF), ms_ref[...])
        at = iota(out.shape, 0) + a
        out = jnp.where((at >= FREQ) & (at < limit), out, 0.0).astype(BF)
        for dx in range(3):
            img[dx, a : a + step, :] = out[:, dx * S : (dx + 1) * S]
    for m in range(NB):
        for dx in range(3):
            xb[dx * XW : (dx + 1) * XW, m * S : (m + 1) * S] = img[
                dx, m * R * FREQ : m * R * FREQ + XW, :
            ]
    xb[3 * XW :, :] = jnp.ones((CH, LANES), BF)
    zero_edges(hb, 0)
    zero_edges(gp_ref, 0)
    own = (iota((R * CH, CH), 0) & 15) == iota((R * CH, CH), 1)
    bias = jnp.sum(jnp.where(own, bias_ref[...], 0.0), axis=1, keepdims=True)
    pairs = jnp.zeros((R * CH, 3 * XW + CH), F32)
    for n in range(0, LANES, 2 * S):
        pre = dot(t1_ref[...], xb[:, n : n + 2 * S]) + bias
        gate = jax.nn.sigmoid(pre)
        hidden = (pre * gate).astype(BF)
        grad = (gh_ref[:, n : n + 2 * S] * (gate * (1.0 + pre * (1.0 - gate)))).astype(BF)
        pairs = pairs + dot_t(grad, xb[:, n : n + 2 * S])
        for b in range(2):
            m = n // S + b
            lanes = slice(b * S, (b + 1) * S)
            for ref, value in ((hb, hidden), (gp_ref, grad)):
                ref[CH : CH + R * CH, m * S : (m + 1) * S] = value[:, lanes]
                if m > 0:
                    ref[(R + 1) * CH : WIN, (m - 1) * S : m * S] = value[0:CH, lanes]
                if m < NB - 1:
                    ref[0:CH, (m + 1) * S : (m + 2) * S] = value[(R - 1) * CH :, lanes]
    lane = iota((CH, 2 * S), 1)
    result = jnp.zeros((CH, 2 * S), F32)
    every = dot_t(big_ref[:, 0:LANES], hb[...])
    for dx in range(3):
        g = every[dx * S : (dx + 1) * S, :]
        g = jnp.concatenate([g, jnp.zeros((R * CH, 2 * S - WIN), F32)], axis=1)
        acc = g[0:CH, :]
        for r in range(1, R):
            acc = acc + pltpu.roll(g[r * CH : (r + 1) * CH, :], 2 * S - r * CH, 1)
        if dx:
            acc = pltpu.roll(acc, dx * 3 * CH, 1)
        result = jnp.where((lane >= dx * 3 * CH) & (lane < (dx + 1) * 3 * CH), acc, result)
    g = jnp.concatenate([pairs, jnp.zeros((R * CH, 2 * S - pairs.shape[1]), F32)], axis=1)
    acc = g[0:CH, :]
    ones = g[0:CH, :]
    for r in range(1, R):
        part = g[r * CH : (r + 1) * CH, :]
        ones = ones + part
        acc = acc + pltpu.roll(part, 2 * S - r * FREQ, 1)
    acc = pltpu.roll(acc, 9 * CH, 1)
    ones = pltpu.roll(ones, 2 * S - 1 - 3 * XW, 1)
    result = jnp.where(lane >= 9 * CH, acc, result)
    w_ref[...] = jnp.where(lane == 2 * S - 1, ones, result)


def slots_kernel(rows_ref, gp_ref, big_ref, *refs):
    out_refs, (grad, gsrc) = refs[:-2], refs[-2:]
    height = out_refs[0].shape[0]
    oh_ref, mt_ref, t3_ref, _ = late(big_ref, height * len(out_refs), 0)
    part = R * FREQ
    limit = rows_ref[0, 0]
    pad = 2 * FREQ
    grad[0:pad, :] = jnp.zeros((pad, S), F32)
    end = pad + S * FREQ
    grad[end:, :] = jnp.zeros((grad.shape[0] - end, S), F32)
    for n in range(0, LANES, 4 * S):
        u = dot(t3_ref[...], gp_ref[:, n : n + 4 * S])
        for b in range(4):
            m = n // S + b
            lanes = slice(b * S, (b + 1) * S)
            rows = shifted(u[0:part, lanes], 1) + u[part : 2 * part, lanes]
            rows = rows + shifted(u[2 * part : 3 * part, lanes], -1)
            y = (iota(rows.shape, 0) >> 2) + m * R
            grad[pad + m * part : pad + (m + 1) * part, :] = jnp.where(y < limit, rows, 0.0)
    step = 176
    for a in range(0, 3 * step, step):
        pair = jnp.concatenate(
            [grad[pad + a : pad + a + step, :], grad[FREQ + a : FREQ + a + step, :]], axis=1
        )
        gsrc[a : a + step, :] = dot(pair.astype(BF), mt_ref[...])
    gsrc[3 * step :, :] = jnp.zeros((gsrc.shape[0] - 3 * step, S), F32)
    for f in range(FREQ):
        rows = gsrc[pl.ds(f, SRC, stride=FREQ), :]
        high = rows.astype(BF)
        low = (rows - high.astype(F32)).astype(BF)
        out = dot(oh_ref[...], high) + dot(oh_ref[...], low)
        for d, out_ref in enumerate(out_refs):
            rows = out[d * height : (d + 1) * height, :]
            out_ref[0:height, f * S : (f + 1) * S] = rows.astype(BF)


def split(value):
    high = value.astype(BF)
    return high, (value - high.astype(F32)).astype(BF)


def joined(rows):
    return rows[:, 0 : 2 * S].astype(F32) + rows[:, 2 * S : 4 * S].astype(F32)


def pack_kernel(w_ref, *refs):
    count = (len(refs) - 2) // 2
    out_refs, (packed, sems) = refs[count:-2], refs[-2:]
    packed[:, 0 : 2 * S], packed[:, 2 * S : 4 * S] = split(w_ref[...])
    pairs = [(packed, ref.at[pl.ds(ref.shape[0] - CH, CH), :]) for ref in out_refs]
    for copy in fetch(pairs, sems):
        copy.wait()


def relay_kernel(w_ref, own_ref, *refs):
    in_refs, (out_ref, sum_ref) = refs[:-2], refs[-2:]
    pair = own_ref.shape[0]
    capacity = pair // 2
    high, low = split(w_ref[...])
    terms = [high.astype(F32) + low.astype(F32)]
    for d, ref in enumerate((own_ref, *in_refs)):
        out_ref[d * capacity : (d + 1) * capacity, :] = ref[capacity:pair, :]
        if d:
            terms.append(joined(ref[pair : pair + CH, :]))
    terms[1:] = terms[:0:-1]
    while len(terms) > 1:
        terms = [a + b for a, b in zip(terms[0::2], terms[1::2])]
    high, low = split(terms[0])
    sum_ref[...] = high.astype(F32) + low.astype(F32)
    at = out_ref.shape[0] - CH
    out_ref[at:, 0 : 2 * S] = high
    out_ref[at:, 2 * S : 4 * S] = low


def final_kernel(scale, big_ref, sum_ref, *refs):
    in_refs, far_ref, (map_ref, w1_ref, bias_ref, w2_ref) = refs[:-5], refs[-5], refs[-4:]
    blocks = map_ref.shape[0]
    capacity = in_refs[0].shape[0] // 2
    middle = capacity * len(in_refs)
    sel = late(big_ref, 2 * middle, blocks)[-1][...]
    near = jnp.concatenate([ref[0:capacity, :] for ref in in_refs], axis=0)
    total = dot(sel, jnp.concatenate([near, far_ref[0:middle, :]], axis=0))
    for f in range(FREQ):
        map_ref[:, f, :] = total[:, f * S : (f + 1) * S]
    weights = (sum_ref[...] + joined(far_ref[middle:, :])) * scale
    for dy in range(3):
        for dx in range(3):
            at = (dx * 3 + dy) * CH
            w2_ref[dy * 3 + dx] = weights[:, at : at + CH]
    flat = jnp.concatenate([weights[:, S:], jnp.zeros((S - CH, S), F32)], axis=0).T
    for dy in range(3):
        for dx in range(3):
            at = 9 * CH - S + dx * XW + dy * FREQ
            w1_ref[dy * 3 + dx] = flat[at : at + FREQ, 0:CH]
    bias_ref[...] = flat[S - 1 : S, 0:CH]


def vmem(n):
    return [pl.BlockSpec(memory_space=pltpu.VMEM)] * n


def hbm(n):
    return [pl.BlockSpec(memory_space=pl.ANY)] * n


def smem(n):
    return [pl.BlockSpec(memory_space=pltpu.SMEM)] * n


def call(kernel, out_shape, in_specs, out_specs, scratch=(), **extra):
    return pl.pallas_call(
        kernel,
        out_shape=out_shape,
        in_specs=in_specs,
        out_specs=out_specs,
        scratch_shapes=list(scratch),
        compiler_params=pltpu.CompilerParams(vmem_limit_bytes=VMEM_LIMIT),
        **extra,
    )


def arr(shape, dtype):
    return jax.ShapeDtypeStruct(shape, dtype)


def in_hbm(*values):
    return [pltpu.with_memory_space_constraint(value, pltpu.HBM) for value in values]


def in_vmem(*values):
    return [pltpu.with_memory_space_constraint(value, pltpu.VMEM) for value in values]


def band_sum(value, count, beside):
    if count & (count - 1):
        return lax.psum(value, "band"), beside
    step = 1
    while step < count:
        pairs = [(i, i ^ step) for i in range(count)]
        value = value + lax.ppermute(value, "band", pairs)
        if step == 1:
            value, beside = lax.optimization_barrier((value, beside))
        step *= 2
    return value, beside


def to_chips(values, count):
    chips = count // 2
    return [
        lax.ppermute(value, "tile", [(i, i ^ (2 * (chips - p))) for i in range(count)])
        for p, value in enumerate(values, 1)
    ]


def to_core(value, count):
    return lax.ppermute(value, "tile", [(i, i ^ 1) for i in range(count)])


def shards(
    pixel_map,
    interp_bands,
    conv1_weight,
    conv1_bias,
    conv2_weight,
    send_rows,
    patch_slots,
    patch_rows,
    cotangent,
):
    tile_count = lax.axis_size("tile")
    band_count = lax.axis_size("band")
    band_index = lax.axis_index("band")
    owned = pixel_map[0]
    blocks = owned.shape[0]
    send = send_rows[0, 0]
    capacity = send.shape[1]
    chips = tile_count // 2
    slots = patch_slots[0]
    cot = cotangent.reshape(CH * S, S)

    me = lax.axis_index("tile").astype(I32).reshape(1)
    outgoing = call(
        outgoing_kernel,
        [arr((2 * capacity, FREQ, S), BF)] * chips,
        smem(1) + hbm(2),
        vmem(chips),
        (
            pltpu.SMEM(send.shape, I32),
            pltpu.VMEM(owned.shape, BF),
            pltpu.SemaphoreType.DMA((2,)),
        ),
    )(me, *in_hbm(send, owned))
    received = [outgoing[0]] + to_chips(outgoing[1:], tile_count)
    is_polar = jnp.logical_or(
        band_index < band_count // 4, band_index >= band_count - band_count // 4
    )
    polar = is_polar.astype(I32).reshape(1)
    w1 = jnp.transpose(conv1_weight, (2, 3, 1, 0)).reshape(9, FREQ, CH)
    w2 = jnp.transpose(conv2_weight, (2, 3, 0, 1)).reshape(9, CH, CH)
    bias = conv1_bias.reshape(1, CH)
    cost = pl.CostEstimate(flops=4 * 10**9, bytes_accessed=4 * 10**6, transcendentals=0)
    big, gh, picks = call(
        functools.partial(prepare_kernel, chips, capacity),
        (
            pltpu.VMEM((3 * S, LANES + 3 * S), BF),
            pltpu.VMEM((R * CH, LANES), F32),
            pltpu.SMEM((1, 2 * SRC), I32),
        ),
        smem(2) + hbm(5),
        vmem(2) + smem(1),
        (
            pltpu.SMEM(slots.shape, I32),
            pltpu.VMEM((3 * WIN, LANES), BF),
            pltpu.VMEM((CH * S, S), F32),
            pltpu.VMEM((R * CH, 3 * WIN), BF),
            pltpu.VMEM(cot.shape, BF),
            pltpu.VMEM(w1.shape, BF),
            pltpu.VMEM(w2.shape, BF),
            pltpu.VMEM(interp_bands.shape, BF),
            pltpu.VMEM((9 * FREQ, CH), F32),
            pltpu.VMEM((9 * CH, CH), F32),
            pltpu.SemaphoreType.DMA((5,)),
        ),
        cost_estimate=cost,
    )(polar, me, *in_hbm(cot, w1, w2, interp_bands, slots))

    big, *received = lax.optimization_barrier((big, *received))
    blocks_half = pltpu.VMEM((chips * capacity, FREQ, S), BF)
    relayed = call(functools.partial(half_kernel, 1), blocks_half, vmem(chips), vmem(1)[0])(*received)
    far = to_core(relayed, tile_count)
    near = call(functools.partial(half_kernel, 0), blocks_half, vmem(chips), vmem(1)[0])(*received)

    padded = (S + 4) * FREQ
    weights, gp = call(
        functools.partial(patch_kernel, slots.shape[1]),
        (pltpu.VMEM((CH, 2 * S), F32), pltpu.VMEM((WIN, LANES), BF)),
        smem(2) + vmem(5),
        vmem(2),
        (
            pltpu.VMEM((padded + 8, S), F32),
            pltpu.VMEM((3, padded, S), BF),
            pltpu.VMEM((3 * XW + CH, LANES), BF),
            pltpu.VMEM((WIN, LANES), BF),
        ),
    )(picks, patch_rows, bias, near, far, *in_vmem(big, gh))

    rows = max(3 * S, tile_count * capacity)
    lists = call(
        functools.partial(lists_kernel, blocks),
        pltpu.VMEM((rows, 4 * S + tile_count * capacity), BF),
        smem(2) + hbm(5),
        vmem(1)[0],
        (
            pltpu.VMEM((1, tile_count * capacity), I32),
            pltpu.VMEM(w1.shape, BF),
            pltpu.VMEM(interp_bands.shape, BF),
            pltpu.VMEM(slots.shape, I32),
            pltpu.VMEM(send.shape, I32),
            pltpu.VMEM((9 * FREQ, CH), F32),
            pltpu.SemaphoreType.DMA((4,)),
        ),
        cost_estimate=cost,
    )(polar, me, *in_hbm(w1, interp_bands, slots, send), gp)
    weights, lists = band_sum(weights, band_count, lists)
    pair = 2 * capacity
    full = arr((pair + CH, 4 * S), BF)
    returning = call(
        slots_kernel,
        [arr((pair, 4 * S), BF)] + [full] * (chips - 1),
        smem(1) + vmem(2),
        vmem(chips),
        (pltpu.VMEM((padded + 16, S), F32), pltpu.VMEM((SRC * FREQ, S), F32)),
    )(patch_rows, *in_vmem(gp, lists))
    own = returning[0]
    packed = call(
        pack_kernel,
        [full] * (chips - 1),
        vmem(1) + hbm(chips - 1),
        hbm(chips - 1),
        (pltpu.VMEM((CH, 4 * S), BF), pltpu.SemaphoreType.DMA((chips - 1,))),
        input_output_aliases={i: i - 1 for i in range(1, chips)},
    )(weights, *returning[1:])
    returned = to_chips(packed, tile_count)
    relayed, total = call(
        relay_kernel,
        (arr((chips * capacity + CH, 4 * S), BF), arr((CH, 2 * S), F32)),
        vmem(1 + chips),
        vmem(2),
    )(weights, own, *returned)
    back = to_core(relayed, tile_count)
    norm_scale = float(band_count * tile_count * S * S) ** (-0.5)
    grad_map, grad1, grad_bias, grad2 = call(
        functools.partial(final_kernel, norm_scale),
        (
            arr((blocks, FREQ, S), F32),
            arr((9, FREQ, CH), F32),
            arr((1, CH), F32),
            arr((9, CH, CH), F32),
        ),
        vmem(3 + chips),
        vmem(4),
    )(*in_vmem(lists), total, own, *returned, back)
    return (
        grad_map[None],
        jnp.transpose(grad1.reshape(3, 3, FREQ, CH), (3, 2, 0, 1)),
        grad_bias.reshape(CH),
        jnp.transpose(grad2.reshape(3, 3, CH, CH), (2, 3, 0, 1)),
    )


def solution(mesh):
    in_specs = (
        P("band", "tile", None, None),
        P(),
        P(),
        P(),
        P(),
        P("band", "tile", None, None),
        P("band", "tile", None),
        P("band", "tile"),
        P("band", "tile", None, None, None),
    )
    out_specs = (P("band", "tile", None, None), P(), P(), P())
    return jax.shard_map(shards, mesh=mesh, in_specs=in_specs, out_specs=out_specs, check_vma=False)
```

```python
import functools

import jax
import jax.numpy as jnp
from jax import lax
from jax.experimental import pallas as pl
from jax.experimental.pallas import tpu as pltpu
from jax.sharding import PartitionSpec as P

BF = jnp.bfloat16
F32 = jnp.float32
I32 = jnp.int32
S = 128
FREQ = 4
CH = 16
R = 8
NB = S // R
WIN = (R + 2) * CH
XW = 48
LANES = NB * S
SRC = 144
VMEM_LIMIT = 16 * 1024 * 1024


def iota(shape, axis):
    return lax.broadcasted_iota(I32, shape, axis)


def dot(a, b):
    return lax.dot_general(a, b, (((1,), (0,)), ((), ())), preferred_element_type=F32)


def dot_t(a, b):
    return lax.dot_general(a, b, (((1,), (1,)), ((), ())), preferred_element_type=F32)


def shifted(rows, step):
    lane = iota(rows.shape, 1)
    if step == 1:
        return jnp.where(lane == S - 1, 0.0, pltpu.roll(rows, S - 1, 1))
    return jnp.where(lane == 0, 0.0, pltpu.roll(rows, 1, 1))


def store_window(ref, base, y, tile):
    block, r = divmod(y, R)
    ref[base + (r + 1) * CH : base + (r + 2) * CH, block * S : (block + 1) * S] = tile
    if r == 0 and block > 0:
        ref[base + (R + 1) * CH : base + WIN, (block - 1) * S : block * S] = tile
    if r == R - 1 and block < NB - 1:
        ref[base : base + CH, (block + 1) * S : (block + 2) * S] = tile


def zero_edges(ref, base):
    zero = jnp.zeros((CH, S), BF)
    ref[base : base + CH, 0:S] = zero
    ref[base + (R + 1) * CH : base + WIN, LANES - S : LANES] = zero


class View:
    def __init__(self, ref, row, rows, lane, lanes):
        self.ref, self.origin, self.shape = ref, (row, lane), (rows, lanes)

    def place(self, key):
        key = (slice(None), slice(None)) if key is Ellipsis else key
        spans = [k.indices(n) for k, n in zip(key, self.shape)]
        return tuple(slice(o + a, o + b) for o, (a, b, _) in zip(self.origin, spans))

    def __getitem__(self, key):
        return self.ref[self.place(key)]

    def __setitem__(self, key, value):
        self.ref[self.place(key)] = value


def early(ref):
    return (
        View(ref, 2 * S, R * CH, LANES, 3 * XW + CH),
        View(ref, 0, 2 * S, LANES, 3 * S),
        View(ref, 0, R * CH, LANES + 3 * S, 3 * WIN),
    )


def late(ref, chunks, blocks):
    return (
        View(ref, 0, chunks, 0, SRC),
        View(ref, 0, 2 * S, 2 * S, S),
        View(ref, 2 * S, 3 * R * FREQ, 2 * S, WIN),
        View(ref, 0, blocks, 4 * S, chunks),
    )


def spot(d, chips):
    return -d & (chips - 1)


def fetch(pairs, sems):
    copies = [pltpu.make_async_copy(a, b, sems.at[i]) for i, (a, b) in enumerate(pairs)]
    for copy in copies:
        copy.start()
    return copies


def outgoing_kernel(me_ref, send_hbm, map_hbm, *refs):
    out_refs, (rows_ref, map_ref, sems) = refs[:-3], refs[-3:]
    capacity = rows_ref.shape[1]
    for copy in fetch(((send_hbm, rows_ref), (map_hbm, map_ref)), sems):
        copy.wait()
    chips = len(out_refs)
    for j in range(2 * chips):
        t = me_ref[0] ^ j
        for c in range(capacity):
            out_refs[spot(j // 2, chips)][(j % 2) * capacity + c] = map_ref[rows_ref[t, c]]


def half_kernel(half, *refs):
    out_ref = refs[-1]
    capacity = refs[0].shape[0] // 2
    for d, ref in enumerate(refs[:-1]):
        out_ref[d * capacity : (d + 1) * capacity] = ref[half * capacity : (half + 1) * capacity]


def prepare_kernel(
    chips,
    capacity,
    polar_ref,
    me_ref,
    cot_hbm,
    w1_hbm,
    w2_hbm,
    interp_hbm,
    slots_hbm,
    big_ref,
    picks_ref,
    slots_ref,
    plane,
    cot_ref,
    w1_ref,
    w2_ref,
    interp_ref,
    stack1,
    stack2,
    sems,
):
    copies = fetch(
        (
            (w1_hbm, w1_ref),
            (w2_hbm, w2_ref),
            (interp_hbm, interp_ref),
            (slots_hbm, slots_ref),
            (cot_hbm, cot_ref),
        ),
        sems,
    )
    t1_ref, ms_ref, t2_ref = early(big_ref)
    for copy in copies[:-1]:
        copy.wait()
    for i in range(9):
        stack1[i * FREQ : (i + 1) * FREQ, :] = w1_ref[i].astype(F32)
        stack2[i * CH : (i + 1) * CH, :] = w2_ref[i].astype(F32)
    pick = ((iota((R * CH, CH), 0) & 15) == iota((R * CH, CH), 1)).astype(BF)
    spread = dot_t(pick, stack2[...].astype(BF)).astype(BF)
    row, col = iota((R * CH, 3 * WIN), 0), iota((R * CH, 3 * WIN), 1)
    gap = ((col - jnp.where(col >= 2 * WIN, 2 * WIN, jnp.where(col >= WIN, WIN, 0))) >> 4) - (row >> 4)
    k, kcol = iota((CH * 9, 3 * WIN), 0), iota((CH * 9, 3 * WIN), 1)
    kdx = jnp.where(kcol >= 2 * WIN, 2, jnp.where(kcol >= WIN, 1, 0))
    source = kdx * CH + (kcol & 15)
    banded = jnp.zeros((R * CH, 3 * WIN), F32)
    for dy in range(3):
        term = dot(spread, (k == source + dy * 3 * CH).astype(BF))
        banded = jnp.where(gap == 2 - dy, term, banded)
    t2_ref[...] = banded.astype(BF)
    weights1 = stack1[...].astype(BF)
    spread = dot_t(pick, weights1).astype(BF)
    width = 3 * XW + CH
    row, col = iota((R * CH, width), 0), iota((R * CH, width), 1)
    cdx = jnp.where(col >= 3 * XW, 3, jnp.where(col >= 2 * XW, 2, jnp.where(col >= XW, 1, 0)))
    gap = ((col - cdx * XW) >> 2) - (row >> 4)
    gap = jnp.where(cdx == 3, -1, gap)
    k, kcol = iota((FREQ * 9, width), 0), iota((FREQ * 9, width), 1)
    kdx = jnp.where(kcol >= 3 * XW, 3, jnp.where(kcol >= 2 * XW, 2, jnp.where(kcol >= XW, 1, 0)))
    source = kdx * FREQ + (kcol & 3)
    banded = jnp.zeros((R * CH, width), F32)
    for dy in range(3):
        term = dot(spread, (k == source + dy * 3 * FREQ).astype(BF))
        banded = jnp.where(gap == dy, term, banded)
    t1_ref[...] = banded.astype(BF)

    for half in range(2):
        matrix = jnp.where(
            polar_ref[0] == 1, interp_ref[0, half].astype(F32), interp_ref[1, half].astype(F32)
        )
        at = slice(half * S, (half + 1) * S)
        ms_ref[at, 0:S] = shifted(matrix, -1).astype(BF)
        ms_ref[at, S : 2 * S] = matrix.astype(BF)
        ms_ref[at, 2 * S : 3 * S] = shifted(matrix, 1).astype(BF)

    half = picks_ref.shape[1] // 2
    for k in range(slots_ref.shape[1]):
        slot = slots_ref[0, k]
        if capacity & (capacity - 1):
            owner = lax.div(slot, capacity)
        else:
            owner = slot >> (capacity.bit_length() - 1)
        j = owner ^ me_ref[0]
        picks_ref[0, k] = j & 1
        picks_ref[0, half + k] = (spot(j >> 1, chips) - owner) * capacity + slot

    copies[-1].wait()
    for o in range(CH):
        plane[o * S : (o + 1) * S, :] = cot_ref[o * S : (o + 1) * S, :].astype(F32)
    for dx in range(3):
        zero_edges(big_ref, dx * WIN)
    for y in range(S):
        rows = plane[pl.ds(y, CH, stride=S), :]
        for dx, tile in enumerate((shifted(rows, 1), rows, shifted(rows, -1))):
            store_window(big_ref, dx * WIN, y, tile.astype(BF))


def hidden_kernel(big_ref, gh_ref):
    banded = early(big_ref)[-1][...]
    for n in range(0, LANES, 512):
        gh_ref[:, n : n + 512] = dot(banded, big_ref[0 : 3 * WIN, n : n + 512])


def lists_kernel(
    blocks,
    polar_ref,
    me_ref,
    w1_hbm,
    interp_hbm,
    slots_hbm,
    send_hbm,
    after_hbm,
    big_ref,
    lists,
    w1_ref,
    interp_ref,
    slots_ref,
    send_ref,
    stack1,
    sems,
):
    del after_hbm
    pairs = (
        (w1_hbm, w1_ref),
        (interp_hbm, interp_ref),
        (slots_hbm, slots_ref),
        (send_hbm, send_ref),
    )
    for copy in fetch(pairs, sems):
        copy.wait()
    owners, capacity = send_ref.shape
    nsrc = slots_ref.shape[1]
    oh_ref, mt_ref, t3_ref, sel_ref = late(big_ref, owners * capacity, blocks)
    for i in range(9):
        stack1[i * FREQ : (i + 1) * FREQ, :] = w1_ref[i].astype(F32)
    weights1 = stack1[...].astype(BF)
    part = R * FREQ
    tall = 3 * part
    row, k = iota((tall, FREQ * 9), 0), iota((tall, FREQ * 9), 1)
    rdx = jnp.where(row >= 2 * part, 2, jnp.where(row >= part, 1, 0))
    source = rdx * FREQ + (row & 3)
    column = ((iota((CH, WIN), 1) & 15) == iota((CH, WIN), 0)).astype(BF)
    row, col = iota((tall, WIN), 0), iota((tall, WIN), 1)
    gap = (col >> 4) - ((row & (part - 1)) >> 2)
    banded = jnp.zeros((tall, WIN), F32)
    for dy in range(3):
        spread = dot((k == source + dy * 3 * FREQ).astype(BF), weights1).astype(BF)
        banded = jnp.where(gap == 2 - dy, dot(spread, column), banded)
    t3_ref[...] = banded.astype(BF)

    for half in range(2):
        matrix = jnp.where(
            polar_ref[0] == 1, interp_ref[0, half].astype(F32), interp_ref[1, half].astype(F32)
        )
        mt_ref[half * S : (half + 1) * S, :] = matrix.T.astype(BF)

    slots = jnp.concatenate([slots_ref[...], jnp.full((1, SRC - nsrc), -1, I32)], axis=1)
    for j in range(owners):
        t = me_ref[0] ^ j
        c = iota((capacity, SRC), 0)
        hit = jnp.where(c + t * capacity == slots, 1.0, 0.0)
        place = spot(j // 2, owners // 2)
        at = (2 * place + j % 2) * capacity
        oh_ref[at : at + capacity, :] = hit.astype(BF)
        at = ((j % 2) * (owners // 2) + place) * capacity
        lists[0:1, at : at + capacity] = send_ref[pl.ds(t, 1), :]
    hit = lists[...] == iota(sel_ref.shape, 0)
    sel_ref[...] = jnp.where(hit, 1.0, 0.0).astype(BF)


def patch_kernel(
    nsrc,
    picks_ref,
    rows_ref,
    bias_ref,
    near_ref,
    far_ref,
    big_ref,
    gh_ref,
    w_ref,
    gp_ref,
    src,
    img,
    xb,
    hb,
):
    half = picks_ref.shape[1] // 2
    total = src.shape[0]
    t1_ref, ms_ref, _ = early(big_ref)
    src[0:FREQ, :] = jnp.zeros((FREQ, S), F32)
    first = FREQ * (nsrc + 1)
    src[first:total, :] = jnp.zeros((total - first, S), F32)
    for k in range(nsrc):
        at = picks_ref[0, half + k]
        block = jnp.where(picks_ref[0, k] == 0, near_ref[at].astype(F32), far_ref[at].astype(F32))
        src[FREQ * (k + 1) : FREQ * (k + 2), :] = block
    limit = FREQ * (rows_ref[0, 0] + 1)
    step = img.shape[1] // 3
    for a in range(0, img.shape[1], step):
        pair = jnp.concatenate([src[a : a + step, :], src[a + FREQ : a + FREQ + step, :]], axis=1)
        out = dot(pair.astype(BF), ms_ref[...])
        at = iota(out.shape, 0) + a
        out = jnp.where((at >= FREQ) & (at < limit), out, 0.0).astype(BF)
        for dx in range(3):
            img[dx, a : a + step, :] = out[:, dx * S : (dx + 1) * S]
    for m in range(NB):
        for dx in range(3):
            xb[dx * XW : (dx + 1) * XW, m * S : (m + 1) * S] = img[
                dx, m * R * FREQ : m * R * FREQ + XW, :
            ]
    xb[3 * XW :, :] = jnp.ones((CH, LANES), BF)
    zero_edges(hb, 0)
    zero_edges(gp_ref, 0)
    own = (iota((R * CH, CH), 0) & 15) == iota((R * CH, CH), 1)
    bias = jnp.sum(jnp.where(own, bias_ref[...], 0.0), axis=1, keepdims=True)
    pairs = jnp.zeros((R * CH, 3 * XW + CH), F32)
    for n in range(0, LANES, 2 * S):
        pre = dot(t1_ref[...], xb[:, n : n + 2 * S]) + bias
        gate = jax.nn.sigmoid(pre)
        hidden = (pre * gate).astype(BF)
        grad = (gh_ref[:, n : n + 2 * S] * (gate * (1.0 + pre * (1.0 - gate)))).astype(BF)
        pairs = pairs + dot_t(grad, xb[:, n : n + 2 * S])
        for b in range(2):
            m = n // S + b
            lanes = slice(b * S, (b + 1) * S)
            for ref, value in ((hb, hidden), (gp_ref, grad)):
                ref[CH : CH + R * CH, m * S : (m + 1) * S] = value[:, lanes]
                if m > 0:
                    ref[(R + 1) * CH : WIN, (m - 1) * S : m * S] = value[0:CH, lanes]
                if m < NB - 1:
                    ref[0:CH, (m + 1) * S : (m + 2) * S] = value[(R - 1) * CH :, lanes]
    lane = iota((CH, 2 * S), 1)
    result = jnp.zeros((CH, 2 * S), F32)
    middle = [big_ref[dx * WIN + CH : (dx + 1) * WIN - CH, 0:LANES] for dx in range(3)]
    every = dot_t(jnp.concatenate(middle, axis=0), hb[...])
    for dx in range(3):
        g = every[dx * S : (dx + 1) * S, :]
        g = jnp.concatenate([g, jnp.zeros((R * CH, 2 * S - WIN), F32)], axis=1)
        acc = g[0:CH, :]
        for r in range(1, R):
            acc = acc + pltpu.roll(g[r * CH : (r + 1) * CH, :], 2 * S - r * CH, 1)
        if dx:
            acc = pltpu.roll(acc, dx * 3 * CH, 1)
        result = jnp.where((lane >= dx * 3 * CH) & (lane < (dx + 1) * 3 * CH), acc, result)
    g = jnp.concatenate([pairs, jnp.zeros((R * CH, 2 * S - pairs.shape[1]), F32)], axis=1)
    acc = g[0:CH, :]
    ones = g[0:CH, :]
    for r in range(1, R):
        part = g[r * CH : (r + 1) * CH, :]
        ones = ones + part
        acc = acc + pltpu.roll(part, 2 * S - r * FREQ, 1)
    acc = pltpu.roll(acc, 9 * CH, 1)
    ones = pltpu.roll(ones, 2 * S - 1 - 3 * XW, 1)
    result = jnp.where(lane >= 9 * CH, acc, result)
    w_ref[...] = jnp.where(lane == 2 * S - 1, ones, result)


def slots_kernel(rows_ref, gp_ref, big_ref, *refs):
    out_refs, (grad, gsrc) = refs[:-2], refs[-2:]
    height = out_refs[0].shape[0]
    oh_ref, mt_ref, t3_ref, _ = late(big_ref, height * len(out_refs), 0)
    part = R * FREQ
    limit = rows_ref[0, 0]
    pad = 2 * FREQ
    grad[0:pad, :] = jnp.zeros((pad, S), F32)
    end = pad + S * FREQ
    grad[end:, :] = jnp.zeros((grad.shape[0] - end, S), F32)
    for n in range(0, LANES, 4 * S):
        u = dot(t3_ref[...], gp_ref[:, n : n + 4 * S])
        for b in range(4):
            m = n // S + b
            lanes = slice(b * S, (b + 1) * S)
            rows = shifted(u[0:part, lanes], 1) + u[part : 2 * part, lanes]
            rows = rows + shifted(u[2 * part : 3 * part, lanes], -1)
            y = (iota(rows.shape, 0) >> 2) + m * R
            grad[pad + m * part : pad + (m + 1) * part, :] = jnp.where(y < limit, rows, 0.0)
    step = 176
    for a in range(0, 3 * step, step):
        pair = jnp.concatenate(
            [grad[pad + a : pad + a + step, :], grad[FREQ + a : FREQ + a + step, :]], axis=1
        )
        gsrc[a : a + step, :] = dot(pair.astype(BF), mt_ref[...])
    gsrc[3 * step :, :] = jnp.zeros((gsrc.shape[0] - 3 * step, S), F32)
    for f in range(FREQ):
        rows = gsrc[pl.ds(f, SRC, stride=FREQ), :]
        high = rows.astype(BF)
        low = (rows - high.astype(F32)).astype(BF)
        out = dot(oh_ref[...], high) + dot(oh_ref[...], low)
        for d, out_ref in enumerate(out_refs):
            rows = out[d * height : (d + 1) * height, :]
            out_ref[0:height, f * S : (f + 1) * S] = rows.astype(BF)


def split(value):
    high = value.astype(BF)
    return high, (value - high.astype(F32)).astype(BF)


def joined(rows):
    return rows[:, 0 : 2 * S].astype(F32) + rows[:, 2 * S : 4 * S].astype(F32)


def pack_kernel(w_ref, *refs):
    count = (len(refs) - 2) // 2
    out_refs, (packed, sems) = refs[count:-2], refs[-2:]
    packed[:, 0 : 2 * S], packed[:, 2 * S : 4 * S] = split(w_ref[...])
    pairs = [(packed, ref.at[pl.ds(ref.shape[0] - CH, CH), :]) for ref in out_refs]
    for copy in fetch(pairs, sems):
        copy.wait()


def relay_kernel(w_ref, own_ref, *refs):
    in_refs, (out_ref, sum_ref) = refs[:-2], refs[-2:]
    pair = own_ref.shape[0]
    capacity = pair // 2
    high, low = split(w_ref[...])
    terms = [high.astype(F32) + low.astype(F32)]
    for d, ref in enumerate((own_ref, *in_refs)):
        out_ref[d * capacity : (d + 1) * capacity, :] = ref[capacity:pair, :]
        if d:
            terms.append(joined(ref[pair : pair + CH, :]))
    terms[1:] = terms[:0:-1]
    while len(terms) > 1:
        terms = [a + b for a, b in zip(terms[0::2], terms[1::2])]
    high, low = split(terms[0])
    sum_ref[...] = high.astype(F32) + low.astype(F32)
    at = out_ref.shape[0] - CH
    out_ref[at:, 0 : 2 * S] = high
    out_ref[at:, 2 * S : 4 * S] = low


def final_kernel(scale, big_ref, sum_ref, *refs):
    in_refs, far_ref, (map_ref, w1_ref, bias_ref, w2_ref) = refs[:-5], refs[-5], refs[-4:]
    blocks = map_ref.shape[0]
    capacity = in_refs[0].shape[0] // 2
    middle = capacity * len(in_refs)
    sel = late(big_ref, 2 * middle, blocks)[-1][...]
    near = jnp.concatenate([ref[0:capacity, :] for ref in in_refs], axis=0)
    total = dot(sel, jnp.concatenate([near, far_ref[0:middle, :]], axis=0))
    for f in range(FREQ):
        map_ref[:, f, :] = total[:, f * S : (f + 1) * S]
    weights = (sum_ref[...] + joined(far_ref[middle:, :])) * scale
    for dy in range(3):
        for dx in range(3):
            at = (dx * 3 + dy) * CH
            w2_ref[dy * 3 + dx] = weights[:, at : at + CH]
    flat = jnp.concatenate([weights[:, S:], jnp.zeros((S - CH, S), F32)], axis=0).T
    for dy in range(3):
        for dx in range(3):
            at = 9 * CH - S + dx * XW + dy * FREQ
            w1_ref[dy * 3 + dx] = flat[at : at + FREQ, 0:CH]
    bias_ref[...] = flat[S - 1 : S, 0:CH]


def vmem(n):
    return [pl.BlockSpec(memory_space=pltpu.VMEM)] * n


def hbm(n):
    return [pl.BlockSpec(memory_space=pl.ANY)] * n


def smem(n):
    return [pl.BlockSpec(memory_space=pltpu.SMEM)] * n


def call(kernel, out_shape, in_specs, out_specs, scratch=(), **extra):
    return pl.pallas_call(
        kernel,
        out_shape=out_shape,
        in_specs=in_specs,
        out_specs=out_specs,
        scratch_shapes=list(scratch),
        compiler_params=pltpu.CompilerParams(vmem_limit_bytes=VMEM_LIMIT),
        **extra,
    )


def arr(shape, dtype):
    return jax.ShapeDtypeStruct(shape, dtype)


def in_hbm(*values):
    return [pltpu.with_memory_space_constraint(value, pltpu.HBM) for value in values]


def in_vmem(*values):
    return [pltpu.with_memory_space_constraint(value, pltpu.VMEM) for value in values]


def band_sum(value, count, beside):
    if count & (count - 1):
        return lax.psum(value, "band"), beside
    step = 1
    while step < count:
        pairs = [(i, i ^ step) for i in range(count)]
        value = value + lax.ppermute(value, "band", pairs)
        if step == 1:
            value, beside = lax.optimization_barrier((value, beside))
        step *= 2
    return value, beside


def to_chips(values, count):
    chips = count // 2
    return [
        lax.ppermute(value, "tile", [(i, i ^ (2 * (chips - p))) for i in range(count)])
        for p, value in enumerate(values, 1)
    ]


def to_core(value, count):
    return lax.ppermute(value, "tile", [(i, i ^ 1) for i in range(count)])


def shards(
    pixel_map,
    interp_bands,
    conv1_weight,
    conv1_bias,
    conv2_weight,
    send_rows,
    patch_slots,
    patch_rows,
    cotangent,
):
    tile_count = lax.axis_size("tile")
    band_count = lax.axis_size("band")
    band_index = lax.axis_index("band")
    owned = pixel_map[0]
    blocks = owned.shape[0]
    send = send_rows[0, 0]
    capacity = send.shape[1]
    chips = tile_count // 2
    slots = patch_slots[0]
    cot = cotangent.reshape(CH * S, S)

    me = lax.axis_index("tile").astype(I32).reshape(1)
    outgoing = call(
        outgoing_kernel,
        [arr((2 * capacity, FREQ, S), BF)] * chips,
        smem(1) + hbm(2),
        vmem(chips),
        (
            pltpu.SMEM(send.shape, I32),
            pltpu.VMEM(owned.shape, BF),
            pltpu.SemaphoreType.DMA((2,)),
        ),
    )(me, *in_hbm(send, owned))
    received = [outgoing[0]] + to_chips(outgoing[1:], tile_count)
    is_polar = jnp.logical_or(
        band_index < band_count // 4, band_index >= band_count - band_count // 4
    )
    polar = is_polar.astype(I32).reshape(1)
    w1 = jnp.transpose(conv1_weight, (2, 3, 1, 0)).reshape(9, FREQ, CH)
    w2 = jnp.transpose(conv2_weight, (2, 3, 0, 1)).reshape(9, CH, CH)
    bias = conv1_bias.reshape(1, CH)
    cost = pl.CostEstimate(flops=4 * 10**9, bytes_accessed=4 * 10**6, transcendentals=0)
    big, picks = call(
        functools.partial(prepare_kernel, chips, capacity),
        (
            pltpu.VMEM((3 * WIN, LANES + 7 * S), BF),
            pltpu.SMEM((1, 2 * SRC), I32),
        ),
        smem(2) + hbm(5),
        vmem(1) + smem(1),
        (
            pltpu.SMEM(slots.shape, I32),
            pltpu.VMEM((CH * S, S), F32),
            pltpu.VMEM(cot.shape, BF),
            pltpu.VMEM(w1.shape, BF),
            pltpu.VMEM(w2.shape, BF),
            pltpu.VMEM(interp_bands.shape, BF),
            pltpu.VMEM((9 * FREQ, CH), F32),
            pltpu.VMEM((9 * CH, CH), F32),
            pltpu.SemaphoreType.DMA((5,)),
        ),
        cost_estimate=cost,
    )(polar, me, *in_hbm(cot, w1, w2, interp_bands, slots))

    big, *received = lax.optimization_barrier((big, *received))
    blocks_half = pltpu.VMEM((chips * capacity, FREQ, S), BF)
    relayed = call(functools.partial(half_kernel, 1), blocks_half, vmem(chips), vmem(1)[0])(*received)
    far = to_core(relayed, tile_count)
    near = call(functools.partial(half_kernel, 0), blocks_half, vmem(chips), vmem(1)[0])(*received)

    gh = call(
        hidden_kernel, pltpu.VMEM((R * CH, LANES), F32), vmem(1), vmem(1)[0]
    )(*in_vmem(big))
    padded = (S + 4) * FREQ
    weights, gp = call(
        functools.partial(patch_kernel, slots.shape[1]),
        (pltpu.VMEM((CH, 2 * S), F32), pltpu.VMEM((WIN, LANES), BF)),
        smem(2) + vmem(5),
        vmem(2),
        (
            pltpu.VMEM((padded + 8, S), F32),
            pltpu.VMEM((3, padded, S), BF),
            pltpu.VMEM((3 * XW + CH, LANES), BF),
            pltpu.VMEM((WIN, LANES), BF),
        ),
    )(picks, patch_rows, bias, near, far, *in_vmem(big, gh))

    rows = max(3 * S, tile_count * capacity)
    lists = call(
        functools.partial(lists_kernel, blocks),
        pltpu.VMEM((rows, 4 * S + tile_count * capacity), BF),
        smem(2) + hbm(5),
        vmem(1)[0],
        (
            pltpu.VMEM((1, tile_count * capacity), I32),
            pltpu.VMEM(w1.shape, BF),
            pltpu.VMEM(interp_bands.shape, BF),
            pltpu.VMEM(slots.shape, I32),
            pltpu.VMEM(send.shape, I32),
            pltpu.VMEM((9 * FREQ, CH), F32),
            pltpu.SemaphoreType.DMA((4,)),
        ),
        cost_estimate=cost,
    )(polar, me, *in_hbm(w1, interp_bands, slots, send), gp)
    weights, lists = band_sum(weights, band_count, lists)
    pair = 2 * capacity
    full = arr((pair + CH, 4 * S), BF)
    returning = call(
        slots_kernel,
        [arr((pair, 4 * S), BF)] + [full] * (chips - 1),
        smem(1) + vmem(2),
        vmem(chips),
        (pltpu.VMEM((padded + 16, S), F32), pltpu.VMEM((SRC * FREQ, S), F32)),
    )(patch_rows, *in_vmem(gp, lists))
    own = returning[0]
    packed = call(
        pack_kernel,
        [full] * (chips - 1),
        vmem(1) + hbm(chips - 1),
        hbm(chips - 1),
        (pltpu.VMEM((CH, 4 * S), BF), pltpu.SemaphoreType.DMA((chips - 1,))),
        input_output_aliases={i: i - 1 for i in range(1, chips)},
    )(weights, *returning[1:])
    returned = to_chips(packed, tile_count)
    relayed, total = call(
        relay_kernel,
        (arr((chips * capacity + CH, 4 * S), BF), arr((CH, 2 * S), F32)),
        vmem(1 + chips),
        vmem(2),
    )(weights, own, *returned)
    back = to_core(relayed, tile_count)
    norm_scale = float(band_count * tile_count * S * S) ** (-0.5)
    grad_map, grad1, grad_bias, grad2 = call(
        functools.partial(final_kernel, norm_scale),
        (
            arr((blocks, FREQ, S), F32),
            arr((9, FREQ, CH), F32),
            arr((1, CH), F32),
            arr((9, CH, CH), F32),
        ),
        vmem(3 + chips),
        vmem(4),
    )(*in_vmem(lists), total, own, *returned, back)
    return (
        grad_map[None],
        jnp.transpose(grad1.reshape(3, 3, FREQ, CH), (3, 2, 0, 1)),
        grad_bias.reshape(CH),
        jnp.transpose(grad2.reshape(3, 3, CH, CH), (2, 3, 0, 1)),
    )


def solution(mesh):
    in_specs = (
        P("band", "tile", None, None),
        P(),
        P(),
        P(),
        P(),
        P("band", "tile", None, None),
        P("band", "tile", None),
        P("band", "tile"),
        P("band", "tile", None, None, None),
    )
    out_specs = (P("band", "tile", None, None), P(), P(), P())
    return jax.shard_map(shards, mesh=mesh, in_specs=in_specs, out_specs=out_specs, check_vma=False)
```

```python
import functools

import jax
import jax.numpy as jnp
from jax import lax
from jax.experimental import pallas as pl
from jax.experimental.pallas import tpu as pltpu
from jax.sharding import PartitionSpec as P

BF = jnp.bfloat16
F32 = jnp.float32
I32 = jnp.int32
S = 128
FREQ = 4
CH = 16
R = 8
NB = S // R
WIN = (R + 2) * CH
XW = 48
LANES = NB * S
SRC = 144
VMEM_LIMIT = 16 * 1024 * 1024


def iota(shape, axis):
    return lax.broadcasted_iota(I32, shape, axis)


def dot(a, b):
    return lax.dot_general(a, b, (((1,), (0,)), ((), ())), preferred_element_type=F32)


def dot_t(a, b):
    return lax.dot_general(a, b, (((1,), (1,)), ((), ())), preferred_element_type=F32)


def shifted(rows, step):
    lane = iota(rows.shape, 1)
    if step == 1:
        return jnp.where(lane == S - 1, 0.0, pltpu.roll(rows, S - 1, 1))
    return jnp.where(lane == 0, 0.0, pltpu.roll(rows, 1, 1))


def put_block(ref, base, m, tile):
    ref[base + CH : base + CH + R * CH, m * S : (m + 1) * S] = tile
    if m > 0:
        ref[base + (R + 1) * CH : base + WIN, (m - 1) * S : m * S] = tile[0:CH, :]
    if m < NB - 1:
        ref[base : base + CH, (m + 1) * S : (m + 2) * S] = tile[(R - 1) * CH :, :]


def zero_edges(ref, base):
    zero = jnp.zeros((CH, S), BF)
    ref[base : base + CH, 0:S] = zero
    ref[base + (R + 1) * CH : base + WIN, LANES - S : LANES] = zero


class View:
    def __init__(self, ref, row, rows, lane, lanes):
        self.ref, self.origin, self.shape = ref, (row, lane), (rows, lanes)

    def place(self, key):
        key = (slice(None), slice(None)) if key is Ellipsis else key
        spans = [k.indices(n) for k, n in zip(key, self.shape)]
        return tuple(slice(o + a, o + b) for o, (a, b, _) in zip(self.origin, spans))

    def __getitem__(self, key):
        return self.ref[self.place(key)]

    def __setitem__(self, key, value):
        self.ref[self.place(key)] = value


def early(ref):
    return (
        View(ref, 2 * S, R * CH, LANES, 3 * XW + CH),
        View(ref, 0, 2 * S, LANES, 3 * S),
        View(ref, 0, R * CH, LANES + 3 * S, 3 * WIN),
    )


def late(ref, chunks, blocks):
    return (
        View(ref, 0, chunks, 0, SRC),
        View(ref, 0, 2 * S, 2 * S, S),
        View(ref, 2 * S, 3 * R * FREQ, 2 * S, WIN),
        View(ref, 0, blocks, 4 * S, chunks),
    )


def spot(d, chips):
    return -d & (chips - 1)


def fetch(pairs, sems):
    copies = [pltpu.make_async_copy(a, b, sems.at[i]) for i, (a, b) in enumerate(pairs)]
    for copy in copies:
        copy.start()
    return copies


def outgoing_kernel(me_ref, send_hbm, map_hbm, *refs):
    out_refs, (rows_ref, map_ref, sems) = refs[:-3], refs[-3:]
    capacity = rows_ref.shape[1]
    for copy in fetch(((send_hbm, rows_ref), (map_hbm, map_ref)), sems):
        copy.wait()
    chips = len(out_refs)
    for j in range(2 * chips):
        t = me_ref[0] ^ j
        for c in range(capacity):
            out_refs[spot(j // 2, chips)][(j % 2) * capacity + c] = map_ref[rows_ref[t, c]]


def half_kernel(half, *refs):
    out_ref = refs[-1]
    capacity = refs[0].shape[0] // 2
    for d, ref in enumerate(refs[:-1]):
        out_ref[d * capacity : (d + 1) * capacity] = ref[half * capacity : (half + 1) * capacity]


def prepare_kernel(
    chips,
    capacity,
    polar_ref,
    me_ref,
    cot_hbm,
    w1_hbm,
    w2_hbm,
    interp_hbm,
    slots_hbm,
    big_ref,
    picks_ref,
    slots_ref,
    cot_ref,
    w1_ref,
    w2_ref,
    interp_ref,
    stack1,
    stack2,
    sems,
):
    copies = fetch(
        (
            (w1_hbm, w1_ref),
            (w2_hbm, w2_ref),
            (interp_hbm, interp_ref),
            (slots_hbm, slots_ref),
            (cot_hbm, cot_ref),
        ),
        sems,
    )
    t1_ref, ms_ref, t2_ref = early(big_ref)
    for copy in copies[:-1]:
        copy.wait()
    for i in range(9):
        stack1[i * FREQ : (i + 1) * FREQ, :] = w1_ref[i].astype(F32)
        stack2[i * CH : (i + 1) * CH, :] = w2_ref[i].astype(F32)
    pick = ((iota((R * CH, CH), 0) & 15) == iota((R * CH, CH), 1)).astype(BF)
    spread = dot_t(pick, stack2[...].astype(BF)).astype(BF)
    row, col = iota((R * CH, 3 * WIN), 0), iota((R * CH, 3 * WIN), 1)
    gap = ((col - jnp.where(col >= 2 * WIN, 2 * WIN, jnp.where(col >= WIN, WIN, 0))) >> 4) - (row >> 4)
    k, kcol = iota((CH * 9, 3 * WIN), 0), iota((CH * 9, 3 * WIN), 1)
    kdx = jnp.where(kcol >= 2 * WIN, 2, jnp.where(kcol >= WIN, 1, 0))
    source = kdx * CH + (kcol & 15)
    banded = jnp.zeros((R * CH, 3 * WIN), F32)
    for dy in range(3):
        term = dot(spread, (k == source + dy * 3 * CH).astype(BF))
        banded = jnp.where(gap == 2 - dy, term, banded)
    t2_ref[...] = banded.astype(BF)
    weights1 = stack1[...].astype(BF)
    spread = dot_t(pick, weights1).astype(BF)
    width = 3 * XW + CH
    row, col = iota((R * CH, width), 0), iota((R * CH, width), 1)
    cdx = jnp.where(col >= 3 * XW, 3, jnp.where(col >= 2 * XW, 2, jnp.where(col >= XW, 1, 0)))
    gap = ((col - cdx * XW) >> 2) - (row >> 4)
    gap = jnp.where(cdx == 3, -1, gap)
    k, kcol = iota((FREQ * 9, width), 0), iota((FREQ * 9, width), 1)
    kdx = jnp.where(kcol >= 3 * XW, 3, jnp.where(kcol >= 2 * XW, 2, jnp.where(kcol >= XW, 1, 0)))
    source = kdx * FREQ + (kcol & 3)
    banded = jnp.zeros((R * CH, width), F32)
    for dy in range(3):
        term = dot(spread, (k == source + dy * 3 * FREQ).astype(BF))
        banded = jnp.where(gap == dy, term, banded)
    t1_ref[...] = banded.astype(BF)

    for half in range(2):
        matrix = jnp.where(
            polar_ref[0] == 1, interp_ref[0, half].astype(F32), interp_ref[1, half].astype(F32)
        )
        at = slice(half * S, (half + 1) * S)
        ms_ref[at, 0:S] = shifted(matrix, -1).astype(BF)
        ms_ref[at, S : 2 * S] = matrix.astype(BF)
        ms_ref[at, 2 * S : 3 * S] = shifted(matrix, 1).astype(BF)

    half = picks_ref.shape[1] // 2
    for k in range(slots_ref.shape[1]):
        slot = slots_ref[0, k]
        if capacity & (capacity - 1):
            owner = lax.div(slot, capacity)
        else:
            owner = slot >> (capacity.bit_length() - 1)
        j = owner ^ me_ref[0]
        picks_ref[0, k] = j & 1
        picks_ref[0, half + k] = (spot(j >> 1, chips) - owner) * capacity + slot

    copies[-1].wait()
    for dx in range(3):
        zero_edges(big_ref, dx * WIN)
    row, col = iota((R * CH, R * CH), 0), iota((R * CH, R * CH), 1)
    order = (col == (row & 15) * R + (row >> 4)).astype(BF)
    for m in range(NB):
        parts = [cot_ref[o * S + m * R : o * S + (m + 1) * R, :] for o in range(CH)]
        rows = dot(order, jnp.concatenate(parts, axis=0))
        for dx, tile in enumerate((shifted(rows, 1), rows, shifted(rows, -1))):
            put_block(big_ref, dx * WIN, m, tile.astype(BF))


def hidden_kernel(big_ref, gh_ref):
    banded = early(big_ref)[-1][...]
    for n in range(0, LANES, 512):
        gh_ref[:, n : n + 512] = dot(banded, big_ref[0 : 3 * WIN, n : n + 512])


def lists_kernel(
    blocks,
    polar_ref,
    me_ref,
    w1_hbm,
    interp_hbm,
    slots_hbm,
    send_hbm,
    after_hbm,
    big_ref,
    lists,
    w1_ref,
    interp_ref,
    slots_ref,
    send_ref,
    stack1,
    sems,
):
    del after_hbm
    pairs = (
        (w1_hbm, w1_ref),
        (interp_hbm, interp_ref),
        (slots_hbm, slots_ref),
        (send_hbm, send_ref),
    )
    for copy in fetch(pairs, sems):
        copy.wait()
    owners, capacity = send_ref.shape
    nsrc = slots_ref.shape[1]
    oh_ref, mt_ref, t3_ref, sel_ref = late(big_ref, owners * capacity, blocks)
    for i in range(9):
        stack1[i * FREQ : (i + 1) * FREQ, :] = w1_ref[i].astype(F32)
    weights1 = stack1[...].astype(BF)
    part = R * FREQ
    tall = 3 * part
    row, k = iota((tall, FREQ * 9), 0), iota((tall, FREQ * 9), 1)
    rdx = jnp.where(row >= 2 * part, 2, jnp.where(row >= part, 1, 0))
    source = rdx * FREQ + (row & 3)
    column = ((iota((CH, WIN), 1) & 15) == iota((CH, WIN), 0)).astype(BF)
    row, col = iota((tall, WIN), 0), iota((tall, WIN), 1)
    gap = (col >> 4) - ((row & (part - 1)) >> 2)
    banded = jnp.zeros((tall, WIN), F32)
    for dy in range(3):
        spread = dot((k == source + dy * 3 * FREQ).astype(BF), weights1).astype(BF)
        banded = jnp.where(gap == 2 - dy, dot(spread, column), banded)
    t3_ref[...] = banded.astype(BF)

    for half in range(2):
        matrix = jnp.where(
            polar_ref[0] == 1, interp_ref[0, half].astype(F32), interp_ref[1, half].astype(F32)
        )
        mt_ref[half * S : (half + 1) * S, :] = matrix.T.astype(BF)

    slots = jnp.concatenate([slots_ref[...], jnp.full((1, SRC - nsrc), -1, I32)], axis=1)
    for j in range(owners):
        t = me_ref[0] ^ j
        c = iota((capacity, SRC), 0)
        hit = jnp.where(c + t * capacity == slots, 1.0, 0.0)
        place = spot(j // 2, owners // 2)
        at = (2 * place + j % 2) * capacity
        oh_ref[at : at + capacity, :] = hit.astype(BF)
        at = ((j % 2) * (owners // 2) + place) * capacity
        lists[0:1, at : at + capacity] = send_ref[pl.ds(t, 1), :]
    hit = lists[...] == iota(sel_ref.shape, 0)
    sel_ref[...] = jnp.where(hit, 1.0, 0.0).astype(BF)


def patch_kernel(
    nsrc,
    picks_ref,
    rows_ref,
    bias_ref,
    near_ref,
    far_ref,
    big_ref,
    gh_ref,
    w_ref,
    gp_ref,
    src,
    img,
    xb,
    hb,
):
    half = picks_ref.shape[1] // 2
    total = src.shape[0]
    t1_ref, ms_ref, _ = early(big_ref)
    src[0:FREQ, :] = jnp.zeros((FREQ, S), F32)
    first = FREQ * (nsrc + 1)
    src[first:total, :] = jnp.zeros((total - first, S), F32)
    for k in range(nsrc):
        at = picks_ref[0, half + k]
        block = jnp.where(picks_ref[0, k] == 0, near_ref[at].astype(F32), far_ref[at].astype(F32))
        src[FREQ * (k + 1) : FREQ * (k + 2), :] = block
    limit = FREQ * (rows_ref[0, 0] + 1)
    step = img.shape[1] // 3
    for a in range(0, img.shape[1], step):
        pair = jnp.concatenate([src[a : a + step, :], src[a + FREQ : a + FREQ + step, :]], axis=1)
        out = dot(pair.astype(BF), ms_ref[...])
        at = iota(out.shape, 0) + a
        out = jnp.where((at >= FREQ) & (at < limit), out, 0.0).astype(BF)
        for dx in range(3):
            img[dx, a : a + step, :] = out[:, dx * S : (dx + 1) * S]
    for m in range(NB):
        for dx in range(3):
            xb[dx * XW : (dx + 1) * XW, m * S : (m + 1) * S] = img[
                dx, m * R * FREQ : m * R * FREQ + XW, :
            ]
    xb[3 * XW :, :] = jnp.ones((CH, LANES), BF)
    zero_edges(hb, 0)
    zero_edges(gp_ref, 0)
    own = (iota((R * CH, CH), 0) & 15) == iota((R * CH, CH), 1)
    bias = jnp.sum(jnp.where(own, bias_ref[...], 0.0), axis=1, keepdims=True)
    pairs = jnp.zeros((R * CH, 3 * XW + CH), F32)
    for n in range(0, LANES, 2 * S):
        pre = dot(t1_ref[...], xb[:, n : n + 2 * S]) + bias
        gate = jax.nn.sigmoid(pre)
        hidden = (pre * gate).astype(BF)
        grad = (gh_ref[:, n : n + 2 * S] * (gate * (1.0 + pre * (1.0 - gate)))).astype(BF)
        pairs = pairs + dot_t(grad, xb[:, n : n + 2 * S])
        for b in range(2):
            m = n // S + b
            lanes = slice(b * S, (b + 1) * S)
            for ref, value in ((hb, hidden), (gp_ref, grad)):
                ref[CH : CH + R * CH, m * S : (m + 1) * S] = value[:, lanes]
                if m > 0:
                    ref[(R + 1) * CH : WIN, (m - 1) * S : m * S] = value[0:CH, lanes]
                if m < NB - 1:
                    ref[0:CH, (m + 1) * S : (m + 2) * S] = value[(R - 1) * CH :, lanes]
    lane = iota((CH, 2 * S), 1)
    result = jnp.zeros((CH, 2 * S), F32)
    middle = [big_ref[dx * WIN + CH : (dx + 1) * WIN - CH, 0:LANES] for dx in range(3)]
    every = dot_t(jnp.concatenate(middle, axis=0), hb[...])
    for dx in range(3):
        g = every[dx * S : (dx + 1) * S, :]
        g = jnp.concatenate([g, jnp.zeros((R * CH, 2 * S - WIN), F32)], axis=1)
        acc = g[0:CH, :]
        for r in range(1, R):
            acc = acc + pltpu.roll(g[r * CH : (r + 1) * CH, :], 2 * S - r * CH, 1)
        if dx:
            acc = pltpu.roll(acc, dx * 3 * CH, 1)
        result = jnp.where((lane >= dx * 3 * CH) & (lane < (dx + 1) * 3 * CH), acc, result)
    g = jnp.concatenate([pairs, jnp.zeros((R * CH, 2 * S - pairs.shape[1]), F32)], axis=1)
    acc = g[0:CH, :]
    ones = g[0:CH, :]
    for r in range(1, R):
        part = g[r * CH : (r + 1) * CH, :]
        ones = ones + part
        acc = acc + pltpu.roll(part, 2 * S - r * FREQ, 1)
    acc = pltpu.roll(acc, 9 * CH, 1)
    ones = pltpu.roll(ones, 2 * S - 1 - 3 * XW, 1)
    result = jnp.where(lane >= 9 * CH, acc, result)
    w_ref[...] = jnp.where(lane == 2 * S - 1, ones, result)


def slots_kernel(rows_ref, gp_ref, big_ref, *refs):
    out_refs, (grad, gsrc) = refs[:-2], refs[-2:]
    height = out_refs[0].shape[0]
    oh_ref, mt_ref, t3_ref, _ = late(big_ref, height * len(out_refs), 0)
    part = R * FREQ
    limit = rows_ref[0, 0]
    pad = 2 * FREQ
    grad[0:pad, :] = jnp.zeros((pad, S), F32)
    end = pad + S * FREQ
    grad[end:, :] = jnp.zeros((grad.shape[0] - end, S), F32)
    for n in range(0, LANES, 4 * S):
        u = dot(t3_ref[...], gp_ref[:, n : n + 4 * S])
        for b in range(4):
            m = n // S + b
            lanes = slice(b * S, (b + 1) * S)
            rows = shifted(u[0:part, lanes], 1) + u[part : 2 * part, lanes]
            rows = rows + shifted(u[2 * part : 3 * part, lanes], -1)
            y = (iota(rows.shape, 0) >> 2) + m * R
            grad[pad + m * part : pad + (m + 1) * part, :] = jnp.where(y < limit, rows, 0.0)
    step = 176
    for a in range(0, 3 * step, step):
        pair = jnp.concatenate(
            [grad[pad + a : pad + a + step, :], grad[FREQ + a : FREQ + a + step, :]], axis=1
        )
        gsrc[a : a + step, :] = dot(pair.astype(BF), mt_ref[...])
    gsrc[3 * step :, :] = jnp.zeros((gsrc.shape[0] - 3 * step, S), F32)
    for f in range(FREQ):
        rows = gsrc[pl.ds(f, SRC, stride=FREQ), :]
        high = rows.astype(BF)
        low = (rows - high.astype(F32)).astype(BF)
        out = dot(oh_ref[...], high) + dot(oh_ref[...], low)
        for d, out_ref in enumerate(out_refs):
            rows = out[d * height : (d + 1) * height, :]
            out_ref[0:height, f * S : (f + 1) * S] = rows.astype(BF)


def split(value):
    high = value.astype(BF)
    return high, (value - high.astype(F32)).astype(BF)


def joined(rows):
    return rows[:, 0 : 2 * S].astype(F32) + rows[:, 2 * S : 4 * S].astype(F32)


def pack_kernel(w_ref, *refs):
    count = (len(refs) - 2) // 2
    out_refs, (packed, sems) = refs[count:-2], refs[-2:]
    packed[:, 0 : 2 * S], packed[:, 2 * S : 4 * S] = split(w_ref[...])
    pairs = [(packed, ref.at[pl.ds(ref.shape[0] - CH, CH), :]) for ref in out_refs]
    for copy in fetch(pairs, sems):
        copy.wait()


def relay_kernel(w_ref, own_ref, *refs):
    in_refs, (out_ref, sum_ref) = refs[:-2], refs[-2:]
    pair = own_ref.shape[0]
    capacity = pair // 2
    high, low = split(w_ref[...])
    terms = [high.astype(F32) + low.astype(F32)]
    for d, ref in enumerate((own_ref, *in_refs)):
        out_ref[d * capacity : (d + 1) * capacity, :] = ref[capacity:pair, :]
        if d:
            terms.append(joined(ref[pair : pair + CH, :]))
    terms[1:] = terms[:0:-1]
    while len(terms) > 1:
        terms = [a + b for a, b in zip(terms[0::2], terms[1::2])]
    high, low = split(terms[0])
    sum_ref[...] = high.astype(F32) + low.astype(F32)
    at = out_ref.shape[0] - CH
    out_ref[at:, 0 : 2 * S] = high
    out_ref[at:, 2 * S : 4 * S] = low


def final_kernel(scale, big_ref, sum_ref, *refs):
    in_refs, far_ref, (map_ref, w1_ref, bias_ref, w2_ref) = refs[:-5], refs[-5], refs[-4:]
    blocks = map_ref.shape[0]
    capacity = in_refs[0].shape[0] // 2
    middle = capacity * len(in_refs)
    sel = late(big_ref, 2 * middle, blocks)[-1][...]
    near = jnp.concatenate([ref[0:capacity, :] for ref in in_refs], axis=0)
    total = dot(sel, jnp.concatenate([near, far_ref[0:middle, :]], axis=0))
    for f in range(FREQ):
        map_ref[:, f, :] = total[:, f * S : (f + 1) * S]
    weights = (sum_ref[...] + joined(far_ref[middle:, :])) * scale
    for dy in range(3):
        for dx in range(3):
            at = (dx * 3 + dy) * CH
            w2_ref[dy * 3 + dx] = weights[:, at : at + CH]
    flat = jnp.concatenate([weights[:, S:], jnp.zeros((S - CH, S), F32)], axis=0).T
    for dy in range(3):
        for dx in range(3):
            at = 9 * CH - S + dx * XW + dy * FREQ
            w1_ref[dy * 3 + dx] = flat[at : at + FREQ, 0:CH]
    bias_ref[...] = flat[S - 1 : S, 0:CH]


def vmem(n):
    return [pl.BlockSpec(memory_space=pltpu.VMEM)] * n


def hbm(n):
    return [pl.BlockSpec(memory_space=pl.ANY)] * n


def smem(n):
    return [pl.BlockSpec(memory_space=pltpu.SMEM)] * n


def call(kernel, out_shape, in_specs, out_specs, scratch=(), **extra):
    return pl.pallas_call(
        kernel,
        out_shape=out_shape,
        in_specs=in_specs,
        out_specs=out_specs,
        scratch_shapes=list(scratch),
        compiler_params=pltpu.CompilerParams(vmem_limit_bytes=VMEM_LIMIT),
        **extra,
    )


def arr(shape, dtype):
    return jax.ShapeDtypeStruct(shape, dtype)


def in_hbm(*values):
    return [pltpu.with_memory_space_constraint(value, pltpu.HBM) for value in values]


def in_vmem(*values):
    return [pltpu.with_memory_space_constraint(value, pltpu.VMEM) for value in values]


def band_sum(value, count, beside):
    if count & (count - 1):
        return lax.psum(value, "band"), beside
    step = 1
    while step < count:
        pairs = [(i, i ^ (count // 2 // step)) for i in range(count)]
        value = value + lax.ppermute(value, "band", pairs)
        if step == 1:
            value, beside = lax.optimization_barrier((value, beside))
        step *= 2
    return value, beside


def to_chips(values, count):
    chips = count // 2
    return [
        lax.ppermute(value, "tile", [(i, i ^ (2 * (chips - p))) for i in range(count)])
        for p, value in enumerate(values, 1)
    ]


def to_core(value, count):
    return lax.ppermute(value, "tile", [(i, i ^ 1) for i in range(count)])


def shards(
    pixel_map,
    interp_bands,
    conv1_weight,
    conv1_bias,
    conv2_weight,
    send_rows,
    patch_slots,
    patch_rows,
    cotangent,
):
    tile_count = lax.axis_size("tile")
    band_count = lax.axis_size("band")
    band_index = lax.axis_index("band")
    owned = pixel_map[0]
    blocks = owned.shape[0]
    send = send_rows[0, 0]
    capacity = send.shape[1]
    chips = tile_count // 2
    slots = patch_slots[0]
    cot = cotangent.reshape(CH * S, S)

    me = lax.axis_index("tile").astype(I32).reshape(1)
    outgoing = call(
        outgoing_kernel,
        [arr((2 * capacity, FREQ, S), BF)] * chips,
        smem(1) + hbm(2),
        vmem(chips),
        (
            pltpu.SMEM(send.shape, I32),
            pltpu.VMEM(owned.shape, BF),
            pltpu.SemaphoreType.DMA((2,)),
        ),
    )(me, *in_hbm(send, owned))
    received = [outgoing[0]] + to_chips(outgoing[1:], tile_count)
    is_polar = jnp.logical_or(
        band_index < band_count // 4, band_index >= band_count - band_count // 4
    )
    polar = is_polar.astype(I32).reshape(1)
    w1 = jnp.transpose(conv1_weight, (2, 3, 1, 0)).reshape(9, FREQ, CH)
    w2 = jnp.transpose(conv2_weight, (2, 3, 0, 1)).reshape(9, CH, CH)
    bias = conv1_bias.reshape(1, CH)
    cost = pl.CostEstimate(flops=4 * 10**9, bytes_accessed=4 * 10**6, transcendentals=0)
    big, picks = call(
        functools.partial(prepare_kernel, chips, capacity),
        (
            pltpu.VMEM((3 * WIN, LANES + 7 * S), BF),
            pltpu.SMEM((1, 2 * SRC), I32),
        ),
        smem(2) + hbm(5),
        vmem(1) + smem(1),
        (
            pltpu.SMEM(slots.shape, I32),
            pltpu.VMEM(cot.shape, BF),
            pltpu.VMEM(w1.shape, BF),
            pltpu.VMEM(w2.shape, BF),
            pltpu.VMEM(interp_bands.shape, BF),
            pltpu.VMEM((9 * FREQ, CH), F32),
            pltpu.VMEM((9 * CH, CH), F32),
            pltpu.SemaphoreType.DMA((5,)),
        ),
        cost_estimate=cost,
    )(polar, me, *in_hbm(cot, w1, w2, interp_bands, slots))

    big, *received = lax.optimization_barrier((big, *received))
    blocks_half = pltpu.VMEM((chips * capacity, FREQ, S), BF)
    relayed = call(functools.partial(half_kernel, 1), blocks_half, vmem(chips), vmem(1)[0])(*received)
    far = to_core(relayed, tile_count)
    near = call(functools.partial(half_kernel, 0), blocks_half, vmem(chips), vmem(1)[0])(*received)

    gh = call(
        hidden_kernel, pltpu.VMEM((R * CH, LANES), F32), vmem(1), vmem(1)[0]
    )(*in_vmem(big))
    padded = (S + 4) * FREQ
    weights, gp = call(
        functools.partial(patch_kernel, slots.shape[1]),
        (pltpu.VMEM((CH, 2 * S), F32), pltpu.VMEM((WIN, LANES), BF)),
        smem(2) + vmem(5),
        vmem(2),
        (
            pltpu.VMEM((padded + 8, S), F32),
            pltpu.VMEM((3, padded, S), BF),
            pltpu.VMEM((3 * XW + CH, LANES), BF),
            pltpu.VMEM((WIN, LANES), BF),
        ),
    )(picks, patch_rows, bias, near, far, *in_vmem(big, gh))

    rows = max(3 * S, tile_count * capacity)
    lists = call(
        functools.partial(lists_kernel, blocks),
        pltpu.VMEM((rows, 4 * S + tile_count * capacity), BF),
        smem(2) + hbm(5),
        vmem(1)[0],
        (
            pltpu.VMEM((1, tile_count * capacity), I32),
            pltpu.VMEM(w1.shape, BF),
            pltpu.VMEM(interp_bands.shape, BF),
            pltpu.VMEM(slots.shape, I32),
            pltpu.VMEM(send.shape, I32),
            pltpu.VMEM((9 * FREQ, CH), F32),
            pltpu.SemaphoreType.DMA((4,)),
        ),
        cost_estimate=cost,
    )(polar, me, *in_hbm(w1, interp_bands, slots, send), gp)
    weights, lists = band_sum(weights, band_count, lists)
    pair = 2 * capacity
    full = arr((pair + CH, 4 * S), BF)
    returning = call(
        slots_kernel,
        [arr((pair, 4 * S), BF)] + [full] * (chips - 1),
        smem(1) + vmem(2),
        vmem(chips),
        (pltpu.VMEM((padded + 16, S), F32), pltpu.VMEM((SRC * FREQ, S), F32)),
    )(patch_rows, *in_vmem(gp, lists))
    own = returning[0]
    packed = call(
        pack_kernel,
        [full] * (chips - 1),
        vmem(1) + hbm(chips - 1),
        hbm(chips - 1),
        (pltpu.VMEM((CH, 4 * S), BF), pltpu.SemaphoreType.DMA((chips - 1,))),
        input_output_aliases={i: i - 1 for i in range(1, chips)},
    )(weights, *returning[1:])
    returned = to_chips(packed, tile_count)
    relayed, total = call(
        relay_kernel,
        (arr((chips * capacity + CH, 4 * S), BF), arr((CH, 2 * S), F32)),
        vmem(1 + chips),
        vmem(2),
    )(weights, own, *returned)
    back = to_core(relayed, tile_count)
    norm_scale = float(band_count * tile_count * S * S) ** (-0.5)
    grad_map, grad1, grad_bias, grad2 = call(
        functools.partial(final_kernel, norm_scale),
        (
            arr((blocks, FREQ, S), F32),
            arr((9, FREQ, CH), F32),
            arr((1, CH), F32),
            arr((9, CH, CH), F32),
        ),
        vmem(3 + chips),
        vmem(4),
    )(*in_vmem(lists), total, own, *returned, back)
    return (
        grad_map[None],
        jnp.transpose(grad1.reshape(3, 3, FREQ, CH), (3, 2, 0, 1)),
        grad_bias.reshape(CH),
        jnp.transpose(grad2.reshape(3, 3, CH, CH), (2, 3, 0, 1)),
    )


def solution(mesh):
    in_specs = (
        P("band", "tile", None, None),
        P(),
        P(),
        P(),
        P(),
        P("band", "tile", None, None),
        P("band", "tile", None),
        P("band", "tile"),
        P("band", "tile", None, None, None),
    )
    out_specs = (P("band", "tile", None, None), P(), P(), P())
    return jax.shard_map(shards, mesh=mesh, in_specs=in_specs, out_specs=out_specs, check_vma=False)
```
